32 devices in a mesh: dp: 8 (over y, x, core), ctx: 4 (over z).
Axes of the slice: x: 2, y: 2, z: 4, core: 2. Of those that a mesh axis runs over, the one named last changes fastest.
Arguments:
- inputs: bfloat16 [8, 512, 9216], P('dp', 'ctx'), may hold values from -6 to 6
- block_order: int32 [8], replicated, may hold values from 0 to 7, each once
- w_value: bfloat16 [9216, 128], P('dp'), may hold values from -0.0625 to 0.0625
- query: bfloat16 [8, 512, 2048], P('dp', 'ctx'), may hold values from -6 to 6
- keys: bfloat16 [8, 512, 128], P('dp', 'ctx'), may hold values from -6 to 6
- out_grad: bfloat16 [8, 512, 2048], P('dp', 'ctx'), may hold values from -6 to 6
Outputs:
- attn_out: bfloat16 [8, 512, 2048], P('dp', 'ctx')
- grad_query: bfloat16 [8, 512, 2048], P('dp', 'ctx')
- grad_keys: bfloat16 [8, 512, 128], P('dp', 'ctx')
- grad_w: float32 [9216, 128], P('dp')
The draws below stay inside these ranges and needn't reach their ends.
Inputs may be any that keep to these rules, and one draw needn't show every extreme that they name: `block_order`: a permutation of the block numbers.
All inputs are finite; a program needn't handle non-finite values.
Results may differ from the reference program's by a relative error of at most 0.02.
Values may be sent and summed in bfloat16 or wider, within the bound.
A program may use at most 64 MiB of HBM per device.

```python
import jax
import jax.numpy as jnp
from jax import lax

D = 9216
HD = 128
HQ = 16
BLK = 64
N_BLOCKS = 8
SEQ = 512
N_DP = 8
N_CTX = 4


def draw_keys(key, part):
    noise_key = jax.random.fold_in(key, 77)
    field = jnp.clip(jax.random.normal(noise_key, (N_DP, SEQ, HD)), -6.0, 6.0)
    return field.astype(jnp.bfloat16)


def draw_query(key, part):
    noise_key = jax.random.fold_in(key, 91)
    field = jnp.clip(jax.random.normal(noise_key, (N_DP, SEQ, HQ, HD)), -6.0, 6.0)
    return field.reshape(N_DP, SEQ, HQ * HD).astype(jnp.bfloat16)


def steps_of(key, extent, shards, least, top_value):
    factor_of = 1.0
    for dim, shards_of in shards:
        steps = jax.random.uniform(jax.random.fold_in(jax.random.fold_in(key, 6), dim), (shards_of,), jnp.float32, least / len(shards), top_value / len(shards))
        factor_of = factor_of * jnp.repeat(jnp.exp(steps), extent[dim] // shards_of).reshape((-1,) + (1,) * (len(extent) - 1 - dim))
    return factor_of


def scatter_about(key, dims, spread, most, cuts=(), kind=jnp.bfloat16):
    factor_of = steps_of(key, dims, cuts, -0.22, 0.18) if cuts else 1.0
    array = jax.random.normal(key, dims, jnp.float32) * spread * factor_of
    return jnp.minimum(jnp.maximum(array, -most), most).astype(kind)


def setup_inputs(seed: int = 0) -> dict:
    seeds = jax.random.split(jax.random.key(seed), 7)
    inputs = scatter_about(seeds[0], (N_DP, SEQ, D), 1.0, 6.0, ((0, 8), (1, 4)))
    block_order = jax.random.permutation(seeds[1], N_BLOCKS).astype(jnp.int32)
    w_value = scatter_about(seeds[2], (D, HD), D ** -0.5, 0.0625, ((0, 8),))
    query = draw_query(jax.random.fold_in(seeds[6], 71), 0)
    keys = draw_keys(jax.random.fold_in(seeds[6], 71), 0)
    out_grad = scatter_about(seeds[5], (N_DP, SEQ, HQ * HD), 1.0, 6.0, ((0, 8), (1, 4)))
    return {"inputs": inputs, "block_order": block_order, "w_value": w_value, "query": query, "keys": keys, "out_grad": out_grad}


def reference(inputs, block_order, w_value, query, keys, out_grad):
    held = jnp.arange(SEQ, dtype=jnp.int32)
    place = (block_order[held // BLK] * BLK + held % BLK).astype(jnp.int32)
    place_groups = place.reshape(N_CTX, 2 * BLK)
    place_before = jnp.roll(place_groups, 1, axis=0)
    scale = 1.0 / (HD ** 0.5)

    def window(packed):
        q_group, k_group, v_group, g_group, k_before, v_before, p_group, p_before = packed
        all_keys = jnp.concatenate([k_group, k_before], axis=0)
        all_values = jnp.concatenate([v_group, v_before], axis=0)
        key_place = jnp.concatenate([p_group, p_before], axis=0)
        allowed = key_place[None, :] <= p_group[:, None]
        q_flat = q_group.reshape(2 * BLK * HQ, HD)
        g_flat = g_group.reshape(2 * BLK * HQ, HD)
        scores = jnp.dot(q_flat, all_keys.T, preferred_element_type=jnp.float32) * scale
        scores = scores.reshape(2 * BLK, HQ, 4 * BLK)
        scores = jnp.where(allowed[:, None, :], scores, -1e30)
        top = jnp.max(scores, axis=2, keepdims=True)
        weights = jnp.exp(scores - top)
        prob = (weights / jnp.sum(weights, axis=2, keepdims=True)).reshape(2 * BLK * HQ, 4 * BLK)
        prob_b = prob.astype(jnp.bfloat16)
        result = jnp.dot(prob_b, all_values, preferred_element_type=jnp.float32).astype(jnp.bfloat16)
        delta = jnp.sum(g_flat.astype(jnp.float32) * result.astype(jnp.float32), axis=1, keepdims=True)
        dprob = jnp.dot(g_flat, all_values.T, preferred_element_type=jnp.float32)
        dscore = (prob * (dprob - delta)).astype(jnp.bfloat16)
        dquery = (jnp.dot(dscore, all_keys, preferred_element_type=jnp.float32) * scale).astype(jnp.bfloat16)
        dkeys_pair = jnp.dot(dscore.T, q_flat, preferred_element_type=jnp.float32) * scale
        dvalues_pair = jnp.dot(prob_b.T, g_flat, preferred_element_type=jnp.float32)
        return (result.reshape(2 * BLK, HQ * HD), dquery.reshape(2 * BLK, HQ * HD), dkeys_pair, dvalues_pair)

    def one(total, packed):
        x_rows, q_rows, k_rows, grad_rows = packed
        values = jnp.dot(x_rows, w_value, preferred_element_type=jnp.float32).astype(jnp.bfloat16)
        q_groups = q_rows.reshape(N_CTX, 2 * BLK, HQ * HD)
        g_groups = grad_rows.reshape(N_CTX, 2 * BLK, HQ * HD)
        k_groups = k_rows.reshape(N_CTX, 2 * BLK, HD)
        v_groups = values.reshape(N_CTX, 2 * BLK, HD)
        result, dquery, dkeys_pair, dvalues_pair = lax.map(
            window,
            (q_groups, k_groups, v_groups, g_groups, jnp.roll(k_groups, 1, axis=0),
             jnp.roll(v_groups, 1, axis=0), place_groups, place_before))
        dkeys = dkeys_pair[:, :2 * BLK] + jnp.roll(dkeys_pair[:, 2 * BLK:], -1, axis=0)
        dvalues = dvalues_pair[:, :2 * BLK] + jnp.roll(dvalues_pair[:, 2 * BLK:], -1, axis=0)
        dkeys = dkeys.astype(jnp.bfloat16).reshape(SEQ, HD)
        dvalues = dvalues.astype(jnp.bfloat16).reshape(SEQ, HD)
        total = total + jnp.dot(x_rows.T, dvalues, preferred_element_type=jnp.float32)
        return total, (result.reshape(SEQ, HQ * HD), dquery.reshape(SEQ, HQ * HD), dkeys)

    start = jnp.zeros((D, HD), jnp.float32)
    grad_w, outs = lax.scan(one, start, (inputs, query, keys, out_grad))
    return outs[0], outs[1], outs[2], grad_w
```

```python
import functools

import jax
import jax.numpy as jnp
from jax import lax
from jax.experimental import pallas as pl
from jax.experimental.pallas import tpu as pltpu
from jax.sharding import PartitionSpec as P

MESH = pl.DeviceIdType.MESH
F32 = jnp.float32
BF16 = jnp.bfloat16


def mul16(value):
    return pl.multiple_of(value, 16)


def dot(a, b, ca, cb):
    return lax.dot_general(a, b, (((ca,), (cb,)), ((), ())), preferred_element_type=F32)


def chunk_of(width):
    best = 128
    for size in range(128, 1537, 128):
        if width % size == 0:
            best = size
    return best


def kernel(
    n_dp, n_ctx, group, pieces,
    order, x, w, q, k, g,
    o, dq, dk, gw,
    x2, w_all, k_all, v_all, probs, dv_acc, dk_acc, dvf, dkf, dv2, term, term_r, z_s, z_r, fin,
    send_sem, recv_sem, local_sem,
):
    rows, width = x.shape
    shard, hd = w.shape
    heads = q.shape[1] // hd
    scale = 1.0 / hd**0.5
    chips = n_dp // 2
    aligned = shard % 128 == 0
    me = lax.axis_index("dp")
    z = lax.axis_index("ctx")
    chip, core = me // 2, lax.rem(me, 2)
    sib = me + 1 - 2 * core
    nxt = lax.rem(z + 1, n_ctx)
    prev = lax.rem(z + n_ctx - 1, n_ctx)

    def peer(off):
        return 2 * lax.rem(chip + off, chips) + core

    def source(off):
        return 2 * lax.rem(chip + chips - off, chips) + core

    count = [0]
    sent = []

    def send(src, dst, target):
        at = count[0]
        count[0] += 1
        copy = pltpu.make_async_remote_copy(
            src_ref=src, dst_ref=dst, send_sem=send_sem.at[at], recv_sem=recv_sem.at[at],
            device_id=target, device_id_type=MESH,
        )
        copy.start()
        sent.append(copy)
        return at

    def arrived(ref, at):
        pltpu.make_async_remote_copy(
            src_ref=ref, dst_ref=ref, send_sem=send_sem.at[at], recv_sem=recv_sem.at[at],
            device_id={"dp": sib}, device_id_type=MESH,
        ).wait_recv()

    load = pltpu.make_async_copy(x, x2.at[pl.ds(0, rows)], local_sem)
    load.start()
    k_all[pl.ds(0, rows)] = k[...]

    barrier = pltpu.get_barrier_semaphore()
    for off in range(1, chips):
        pl.semaphore_signal(barrier, inc=1, device_id={"dp": peer(off)}, device_id_type=MESH)
    pl.semaphore_signal(barrier, inc=1, device_id={"dp": sib}, device_id_type=MESH)
    for off in range(1, n_ctx):
        pl.semaphore_signal(
            barrier, inc=1, device_id={"ctx": lax.rem(z + off, n_ctx)}, device_id_type=MESH
        )
    pl.semaphore_wait(barrier, chips + n_ctx - 1)

    keys_at = send(k, k_all.at[pl.ds(rows, rows)], {"ctx": nxt})
    own = pl.ds(mul16(me * shard), shard)
    w_at = [send(w, w_all.at[own], {"dp": peer(off)}) for off in range(1, chips)]
    w_sib_at = [send(w, w_all.at[own], {"dp": sib})]
    x_at = []
    if aligned:
        for j in range(chips):
            cols = pl.ds(pl.multiple_of((2 * j + 1 - core) * shard, 128), shard)
            x_at.append(send(x.at[:, cols], x2.at[pl.ds(rows, rows), cols], {"dp": sib}))
    else:
        x_at.append(send(x, x2.at[pl.ds(rows, rows)], {"dp": sib}))
    w_all[own] = w[...]

    per = order.shape[0] // n_ctx
    blk = rows // per
    span = group * rows
    key_row = lax.broadcasted_iota(jnp.int32, (2 * rows, span), 0)
    q_col = lax.rem(lax.broadcasted_iota(jnp.int32, (2 * rows, span), 1), rows)
    key_place = jnp.zeros((2 * rows, span), jnp.int32)
    q_place = jnp.zeros((2 * rows, span), jnp.int32)
    for b in range(per):
        mine = order[z * per + b]
        theirs = order[prev * per + b]
        key_place = jnp.where(key_row // blk == b, mine * blk + key_row - b * blk, key_place)
        key_place = jnp.where(
            key_row // blk == per + b, theirs * blk + key_row - (per + b) * blk, key_place
        )
        q_place = jnp.where(q_col // blk == b, mine * blk + q_col - b * blk, q_place)
    bias = jnp.where(key_place <= q_place, 0.0, -1e30).astype(F32)

    def stacked(ref, it):
        return jnp.concatenate(
            [
                ref[:, pl.ds(pl.multiple_of((it * group + i) * hd, 128), hd)]
                for i in range(group)
            ],
            axis=0,
        )

    arrived(k_all.at[pl.ds(rows, rows)], keys_at)
    dv_acc[...] = jnp.zeros_like(dv_acc)
    dk_acc[...] = jnp.zeros_like(dk_acc)

    def first(it, carry):
        scores = dot(k_all[...], stacked(q, it), 1, 1) * scale
        scores = jnp.where(bias < 0.0, -1e30, scores)
        top = jnp.max(scores, axis=0, keepdims=True)
        weights = jnp.exp(scores - top)
        prob = weights * (1.0 / jnp.sum(weights, axis=0, keepdims=True))
        probs[it] = prob
        dv_acc[...] += dot(prob.astype(BF16), stacked(g, it), 1, 0)
        return carry

    lax.fori_loop(0, heads // group, first, 0)

    dvf[0] = dv_acc[pl.ds(rows, rows)].astype(BF16)
    at = send(dvf.at[0], dvf.at[1], {"ctx": prev})
    load.wait()
    arrived(dvf.at[1], at)
    dv2[pl.ds(0, rows)] = (dv_acc[pl.ds(0, rows)] + dvf[1].astype(F32)).astype(BF16)
    at = send(dv2.at[pl.ds(0, rows)], dv2.at[pl.ds(rows, rows)], {"dp": sib})
    for j in range(len(x_at)):
        if aligned:
            cols = pl.ds(pl.multiple_of((2 * j + core) * shard, 128), shard)
            arrived(x2.at[pl.ds(rows, rows), cols], x_at[j])
        else:
            arrived(x2.at[pl.ds(rows, rows)], x_at[j])
    arrived(dv2.at[pl.ds(rows, rows)], at)

    def shard_term(index):
        cols = pl.ds(pl.multiple_of(index * shard, 128), shard)
        term[pl.ds(mul16(index * shard), shard)] = dot(x2[:, cols], dv2[...], 0, 0).astype(BF16)

    if aligned:
        for off in range(1, chips):
            shard_term(peer(off))
    else:
        size = chunk_of(width)
        for start in range(0, width, size):
            cols = pl.ds(start, size)
            term[cols] = dot(x2[:, cols], dv2[...], 0, 0).astype(BF16)
    part = shard // pieces

    def piece(step):
        return lax.rem(z + 1 + step, n_ctx) if pieces > 1 else 0

    term_at = []
    for step in range(pieces):
        line = []
        for off in range(1, chips):
            here = pl.ds(mul16(peer(off) * shard + piece(step) * part), part)
            there = pl.ds(mul16(piece(step) * part), part)
            line.append(send(term.at[here], term_r.at[off - 1, there], {"dp": peer(off)}))
        term_at.append(line)
    if aligned:
        shard_term(me)

    for off in range(1, chips):
        came = w_all.at[pl.ds(mul16(source(off) * shard), shard)]
        arrived(came, w_at[off - 1])
        w_sib_at.append(send(came, came, {"dp": sib}))
    for off in range(chips):
        index = source(off) + 1 - 2 * core
        arrived(w_all.at[pl.ds(mul16(index * shard), shard)], w_sib_at[off])
    v_own = pl.ds(0, rows)
    v_far = pl.ds(rows, rows)
    size = chunk_of(width)

    def project(it, total):
        cols = pl.ds(pl.multiple_of(it * size, 128), size)
        return total + dot(x2[pl.ds(0, rows), cols], w_all[cols], 1, 0)

    total = lax.fori_loop(0, width // size, project, jnp.zeros((rows, hd), F32))
    v_all[v_own] = total.astype(BF16)
    at = send(v_all.at[v_own], v_all.at[v_far], {"ctx": nxt})
    arrived(v_all.at[v_far], at)
    v_t = v_all[...].T
    k_t = k_all[...].T

    def second(it, carry):
        prob = probs[it]
        q_rows = stacked(q, it)
        out_t = dot(v_t, prob.astype(BF16), 1, 0)
        dprob = dot(v_all[...], stacked(g, it), 1, 1)
        delta = jnp.sum(prob * dprob, axis=0, keepdims=True)
        dscore = (prob * (dprob - delta)).astype(BF16)
        dk_acc[...] += dot(dscore, q_rows, 1, 0)
        dq_t = dot(k_t, dscore, 1, 0) * scale
        for i in range(group):
            cols = pl.ds(pl.multiple_of((it * group + i) * hd, 128), hd)
            o[:, cols] = out_t[:, i * rows:(i + 1) * rows].T.astype(BF16)
            dq[:, cols] = dq_t[:, i * rows:(i + 1) * rows].T.astype(BF16)
        return carry

    lax.fori_loop(0, heads // group, second, 0)
    dkf[0] = (dk_acc[pl.ds(rows, rows)] * scale).astype(BF16)
    dk_at = send(dkf.at[0], dkf.at[1], {"ctx": prev})

    z_at = []
    for step in range(pieces):
        there = pl.ds(mul16(piece(step) * part), part)
        total = term[pl.ds(mul16(me * shard + piece(step) * part), part)].astype(F32)
        for off in range(1, chips):
            arrived(term_r.at[off - 1, there], term_at[step][off - 1])
            total += term_r[off - 1, there].astype(F32)
        z_s[there] = total.astype(BF16)
        if step < n_ctx - 1 and pieces > 1:
            z_at.append(send(z_s.at[there], z_r.at[z], {"ctx": piece(step)}))
    if pieces == 1:
        for off in range(1, n_ctx):
            z_at.append(send(z_s, z_r.at[z], {"ctx": lax.rem(z + off, n_ctx)}))
    mine = pl.ds(mul16(z * part), part) if pieces > 1 else pl.ds(0, part)
    z_r[z] = z_s[mine]
    arrived(dkf.at[1], dk_at)
    dk[...] = (dk_acc[pl.ds(0, rows)] * scale + dkf[1].astype(F32)).astype(BF16)
    for off in range(1, n_ctx):
        arrived(z_r.at[lax.rem(z + n_ctx - off, n_ctx)], z_at[off - 1])
    total = z_r[0].astype(F32)
    for index in range(1, n_ctx):
        total += z_r[index].astype(F32)
    fin[mine] = total.astype(BF16)
    if pieces > 1:
        f_at = [
            send(fin.at[mine], fin.at[mine], {"ctx": lax.rem(z + off, n_ctx)})
            for off in range(1, n_ctx)
        ]
        for off in range(1, n_ctx):
            index = lax.rem(z + n_ctx - off, n_ctx)
            arrived(fin.at[pl.ds(mul16(index * part), part)], f_at[off - 1])
    gw[...] = fin[...].astype(F32)
    for copy in sent:
        copy.wait_send()


def shards(n_dp, n_ctx, inputs, block_order, w_value, query, keys, out_grad):
    x, q, k, g = inputs[0], query[0], keys[0], out_grad[0]
    rows, width = x.shape
    shard, hd = w_value.shape
    heads = q.shape[1] // hd
    group = 4 if heads % 4 == 0 else 1
    pieces = n_ctx if shard % (16 * n_ctx) == 0 else 1
    part = shard // pieces
    chips = n_dp // 2
    copies = 2 * chips + max(chips, 1) + 8 + (chips - 1) * pieces + 2 * n_ctx
    vmem = pl.BlockSpec(memory_space=pltpu.VMEM)
    o, dq, dk, gw = pl.pallas_call(
        functools.partial(kernel, n_dp, n_ctx, group, pieces),
        out_shape=(
            jax.ShapeDtypeStruct(q.shape, BF16),
            jax.ShapeDtypeStruct(q.shape, BF16),
            jax.ShapeDtypeStruct(k.shape, BF16),
            jax.ShapeDtypeStruct(w_value.shape, F32),
        ),
        in_specs=[
            pl.BlockSpec(memory_space=pltpu.SMEM),
            pl.BlockSpec(memory_space=pl.ANY),
            vmem, vmem, vmem, vmem,
        ],
        out_specs=(vmem, vmem, vmem, vmem),
        scratch_shapes=[
            pltpu.VMEM((2 * rows, width), BF16),
            pltpu.VMEM((width, hd), BF16),
            pltpu.VMEM((2 * rows, hd), BF16),
            pltpu.VMEM((2 * rows, hd), BF16),
            pltpu.VMEM((heads // group, 2 * rows, group * rows), F32),
            pltpu.VMEM((2 * rows, hd), F32),
            pltpu.VMEM((2 * rows, hd), F32),
            pltpu.VMEM((2, rows, hd), BF16),
            pltpu.VMEM((2, rows, hd), BF16),
            pltpu.VMEM((2 * rows, hd), BF16),
            pltpu.VMEM((width, hd), BF16),
            pltpu.VMEM((max(chips - 1, 1), shard, hd), BF16),
            pltpu.VMEM((shard, hd), BF16),
            pltpu.VMEM((n_ctx, part, hd), BF16),
            pltpu.VMEM((shard, hd), BF16),
            pltpu.SemaphoreType.DMA((copies,)),
            pltpu.SemaphoreType.DMA((copies,)),
            pltpu.SemaphoreType.DMA,
        ],
        compiler_params=pltpu.CompilerParams(
            collective_id=0, has_side_effects=True, vmem_limit_bytes=40 * 2**20
        ),
    )(block_order, x, w_value, q, k, g)
    return o[None], dq[None], dk[None], gw


def solution(mesh):
    split = P("dp", "ctx", None)
    return jax.shard_map(
        functools.partial(shards, mesh.shape["dp"], mesh.shape["ctx"]),
        mesh=mesh,
        in_specs=(split, P(), P("dp", None), split, split, split),
        out_specs=(split, split, split, P("dp", None)),
        check_vma=False,
    )
```

```python
import functools

import jax
import jax.numpy as jnp
from jax import lax
from jax.experimental import pallas as pl
from jax.experimental.pallas import tpu as pltpu
from jax.sharding import PartitionSpec as P

MESH = pl.DeviceIdType.MESH
F32 = jnp.float32
BF16 = jnp.bfloat16


def mul16(value):
    return pl.multiple_of(value, 16)


def dot(a, b, ca, cb):
    return lax.dot_general(a, b, (((ca,), (cb,)), ((), ())), preferred_element_type=F32)


def chunk_of(width):
    best = 128
    for size in range(128, 1537, 128):
        if width % size == 0:
            best = size
    return best


def kernel(
    n_dp, n_ctx, group, rounds,
    order_hbm, x, w, q_hbm, k, g_hbm,
    o_hbm, dq_hbm, dk_hbm, fin_hbm,
    o, dq, dk, fin, order, q, g, x2, w_all, k_all, v_all, probs, dv_acc, dk_acc, dvf, dkf, dv2, term, term_r, z_s, z_r,
    send_sem, recv_sem, local_sem,
):
    rows, width = x.shape
    shard, hd = w.shape
    heads = q.shape[1] // hd
    scale = 1.0 / hd**0.5
    chips = n_dp // 2
    pieces = max(rounds, 1) * (n_ctx if rounds else 1)
    part = shard // pieces
    aligned = shard % 128 == 0
    me = lax.axis_index("dp")
    z = lax.axis_index("ctx")
    chip, core = me // 2, lax.rem(me, 2)
    sib = me + 1 - 2 * core
    nxt = lax.rem(z + 1, n_ctx)
    prev = lax.rem(z + n_ctx - 1, n_ctx)

    def peer(off):
        return 2 * lax.rem(chip + off, chips) + core

    def source(off):
        return 2 * lax.rem(chip + chips - off, chips) + core

    count = [0]
    sent = []

    def send(src, dst, target):
        at = count[0]
        count[0] += 1
        copy = pltpu.make_async_remote_copy(
            src_ref=src, dst_ref=dst, send_sem=send_sem.at[at], recv_sem=recv_sem.at[at],
            device_id=target, device_id_type=MESH,
        )
        copy.start()
        sent.append(copy)
        return at

    def arrived(ref, at):
        pltpu.make_async_remote_copy(
            src_ref=ref, dst_ref=ref, send_sem=send_sem.at[at], recv_sem=recv_sem.at[at],
            device_id={"dp": sib}, device_id_type=MESH,
        ).wait_recv()

    own = pl.ds(mul16(me * shard), shard)
    pairs = [
        (order_hbm, order), (k, k_all.at[pl.ds(0, rows)]), (q_hbm, q), (g_hbm, g),
        (x, x2.at[pl.ds(0, rows)]), (w, w_all.at[own]),
    ]
    loads = [
        pltpu.make_async_copy(src, dst, local_sem.at[i]) for i, (src, dst) in enumerate(pairs)
    ]
    for load in loads:
        load.start()

    barrier = pltpu.get_barrier_semaphore()
    for off in range(1, chips):
        pl.semaphore_signal(barrier, inc=1, device_id={"dp": peer(off)}, device_id_type=MESH)
    pl.semaphore_signal(barrier, inc=1, device_id={"dp": sib}, device_id_type=MESH)
    for off in range(1, n_ctx):
        pl.semaphore_signal(
            barrier, inc=1, device_id={"ctx": lax.rem(z + off, n_ctx)}, device_id_type=MESH
        )
    pl.semaphore_wait(barrier, chips + n_ctx - 1)

    keys_at = send(k, k_all.at[pl.ds(rows, rows)], {"ctx": nxt})
    w_at = [send(w, w_all.at[own], {"dp": peer(off)}) for off in range(1, chips)]
    w_sib_at = [send(w, w_all.at[own], {"dp": sib})]
    x_at = []
    if aligned:
        for j in range(chips):
            cols = pl.ds(pl.multiple_of((2 * j + 1 - core) * shard, 128), shard)
            x_at.append(send(x.at[:, cols], x2.at[pl.ds(rows, rows), cols], {"dp": sib}))
    else:
        x_at.append(send(x, x2.at[pl.ds(rows, rows)], {"dp": sib}))
    loads[0].wait()

    per = order.shape[0] // n_ctx
    blk = rows // per
    span = group * rows
    key_row = lax.broadcasted_iota(jnp.int32, (2 * rows, span), 0)
    q_col = lax.rem(lax.broadcasted_iota(jnp.int32, (2 * rows, span), 1), rows)
    key_place = jnp.zeros((2 * rows, span), jnp.int32)
    q_place = jnp.zeros((2 * rows, span), jnp.int32)
    for b in range(per):
        mine = order[z * per + b]
        theirs = order[prev * per + b]
        key_place = jnp.where(key_row // blk == b, mine * blk + key_row - b * blk, key_place)
        key_place = jnp.where(
            key_row // blk == per + b, theirs * blk + key_row - (per + b) * blk, key_place
        )
        q_place = jnp.where(q_col // blk == b, mine * blk + q_col - b * blk, q_place)
    bias = jnp.where(key_place <= q_place, 0.0, -1e30).astype(F32)

    def stacked(ref, it):
        return jnp.concatenate(
            [
                ref[:, pl.ds(pl.multiple_of((it * group + i) * hd, 128), hd)]
                for i in range(group)
            ],
            axis=0,
        )

    for load in loads[1:4]:
        load.wait()
    arrived(k_all.at[pl.ds(rows, rows)], keys_at)
    dv_acc[...] = jnp.zeros_like(dv_acc)
    dk_acc[...] = jnp.zeros_like(dk_acc)

    def first(it, carry):
        scores = dot(k_all[...], stacked(q, it), 1, 1) * scale
        scores = jnp.where(bias < 0.0, -1e30, scores)
        top = jnp.max(scores, axis=0, keepdims=True)
        weights = jnp.exp(scores - top)
        prob = weights * (1.0 / jnp.sum(weights, axis=0, keepdims=True))
        probs[it] = prob
        dv_acc[...] += dot(prob.astype(BF16), stacked(g, it), 1, 0)
        return carry

    lax.fori_loop(0, heads // group, first, 0)

    dvf[0] = dv_acc[pl.ds(rows, rows)].astype(BF16)
    at = send(dvf.at[0], dvf.at[1], {"ctx": prev})
    loads[4].wait()
    arrived(dvf.at[1], at)
    dv2[pl.ds(0, rows)] = (dv_acc[pl.ds(0, rows)] + dvf[1].astype(F32)).astype(BF16)
    at = send(dv2.at[pl.ds(0, rows)], dv2.at[pl.ds(rows, rows)], {"dp": sib})
    for j in range(len(x_at)):
        if aligned:
            cols = pl.ds(pl.multiple_of((2 * j + core) * shard, 128), shard)
            arrived(x2.at[pl.ds(rows, rows), cols], x_at[j])
        else:
            arrived(x2.at[pl.ds(rows, rows)], x_at[j])
    arrived(dv2.at[pl.ds(rows, rows)], at)

    def shard_term(index):
        cols = pl.ds(pl.multiple_of(index * shard, 128), shard)
        term[pl.ds(mul16(index * shard), shard)] = dot(x2[:, cols], dv2[...], 0, 0).astype(BF16)

    if aligned:
        for off in range(1, chips):
            shard_term(peer(off))
    else:
        size = chunk_of(width)
        for start in range(0, width, size):
            cols = pl.ds(start, size)
            term[cols] = dot(x2[:, cols], dv2[...], 0, 0).astype(BF16)
    def piece(index):
        if not rounds:
            return 0
        return (index // n_ctx) * n_ctx + lax.rem(z + 1 + index % n_ctx, n_ctx)

    def piece_rows(index):
        return pl.ds(mul16(piece(index) * part), part)

    term_at = []
    for index in range(pieces):
        line = []
        for off in range(1, chips):
            here = pl.ds(mul16(peer(off) * shard + piece(index) * part), part)
            there = piece_rows(index)
            line.append(send(term.at[here], term_r.at[off - 1, there], {"dp": peer(off)}))
        term_at.append(line)
    if aligned:
        shard_term(me)

    loads[5].wait()
    for off in range(1, chips):
        came = w_all.at[pl.ds(mul16(source(off) * shard), shard)]
        arrived(came, w_at[off - 1])
        w_sib_at.append(send(came, came, {"dp": sib}))
    for off in range(chips):
        index = source(off) + 1 - 2 * core
        arrived(w_all.at[pl.ds(mul16(index * shard), shard)], w_sib_at[off])
    v_own = pl.ds(0, rows)
    v_far = pl.ds(rows, rows)
    size = chunk_of(width)

    def project(it, total):
        cols = pl.ds(pl.multiple_of(it * size, 128), size)
        return total + dot(x2[pl.ds(0, rows), cols], w_all[cols], 1, 0)

    total = lax.fori_loop(0, width // size, project, jnp.zeros((rows, hd), F32))
    v_all[v_own] = total.astype(BF16)
    at = send(v_all.at[v_own], v_all.at[v_far], {"ctx": nxt})

    z_at = []

    def finish_piece(index):
        there = piece_rows(index)
        total = term[pl.ds(mul16(me * shard + piece(index) * part), part)].astype(F32)
        for off in range(1, chips):
            arrived(term_r.at[off - 1, there], term_at[index][off - 1])
            total += term_r[off - 1, there].astype(F32)
        if not rounds:
            z_s[...] = total.astype(BF16)
            z_r[0, z] = z_s[...]
            for off in range(1, n_ctx):
                z_at.append(send(z_s, z_r.at[0, z], {"ctx": lax.rem(z + off, n_ctx)}))
            return
        turn, step = index // n_ctx, index % n_ctx
        if step < n_ctx - 1:
            z_s[there] = total.astype(BF16)
            target = {"ctx": lax.rem(z + 1 + step, n_ctx)}
            z_at.append(send(z_s.at[there], z_r.at[turn, z], target))
        else:
            z_r[turn, z] = total.astype(BF16)

    f_at = []

    def finish_round(turn):
        for off in range(1, n_ctx):
            at = z_at[turn * (n_ctx - 1) + off - 1]
            arrived(z_r.at[turn, lax.rem(z + n_ctx - off, n_ctx)], at)
        total = z_r[turn, 0].astype(F32)
        for index in range(1, n_ctx):
            total += z_r[turn, index].astype(F32)
        if not rounds:
            fin[...] = total.astype(BF16)
            return
        mine = pl.ds(mul16((turn * n_ctx + z) * part), part)
        fin[mine] = total.astype(BF16)
        for off in range(1, n_ctx):
            f_at.append(send(fin.at[mine], fin.at[mine], {"ctx": lax.rem(z + off, n_ctx)}))

    arrived(v_all.at[v_far], at)
    v_t = v_all[...].T
    k_t = k_all[...].T

    def second(it, carry):
        prob = probs[it]
        q_rows = stacked(q, it)
        out_t = dot(v_t, prob.astype(BF16), 1, 0)
        dprob = dot(v_all[...], stacked(g, it), 1, 1)
        delta = jnp.sum(prob * dprob, axis=0, keepdims=True)
        dscore = (prob * (dprob - delta)).astype(BF16)
        dk_acc[...] += dot(dscore, q_rows, 1, 0)
        dq_t = dot(k_t, dscore, 1, 0) * scale
        for i in range(group):
            cols = pl.ds(pl.multiple_of((it * group + i) * hd, 128), hd)
            o[:, cols] = out_t[:, i * rows:(i + 1) * rows].T.astype(BF16)
            dq[:, cols] = dq_t[:, i * rows:(i + 1) * rows].T.astype(BF16)
        return carry

    steps = heads // group
    first_round = n_ctx if rounds else 1
    done = 0
    for it in range(steps):
        second(it, 0)
        upto = first_round * (it + 1) // steps
        for index in range(done, upto):
            finish_piece(index)
        done = upto
    stores = [
        pltpu.make_async_copy(src, dst, local_sem.at[i])
        for i, (src, dst) in enumerate([(o, o_hbm), (dq, dq_hbm), (dk, dk_hbm), (fin, fin_hbm)])
    ]
    stores[0].start()
    stores[1].start()
    dkf[0] = (dk_acc[pl.ds(rows, rows)] * scale).astype(BF16)
    dk_at = send(dkf.at[0], dkf.at[1], {"ctx": prev})
    finish_round(0)
    for turn in range(1, rounds):
        for step in range(n_ctx):
            finish_piece(turn * n_ctx + step)
    arrived(dkf.at[1], dk_at)
    dk[...] = (dk_acc[pl.ds(0, rows)] * scale + dkf[1].astype(F32)).astype(BF16)
    stores[2].start()
    for turn in range(1, rounds):
        finish_round(turn)
    for turn in range(rounds):
        for off in range(1, n_ctx):
            index = turn * n_ctx + lax.rem(z + n_ctx - off, n_ctx)
            theirs = pl.ds(mul16(index * part), part)
            arrived(fin.at[theirs], f_at[turn * (n_ctx - 1) + off - 1])
    stores[3].start()
    for copy in sent:
        copy.wait_send()
    for copy in stores:
        copy.wait()


def finish(o, dq, dk, fin, o_out, dq_out, dk_out, gw, narrow, wide, sem):
    copies = [
        pltpu.make_async_copy(src, dst, sem.at[i])
        for i, (src, dst) in enumerate([(fin, narrow), (o, o_out), (dq, dq_out), (dk, dk_out)])
    ]
    for copy in copies:
        copy.start()
    copies[0].wait()
    wide[...] = narrow[...].astype(F32)
    last = pltpu.make_async_copy(wide, gw, sem.at[4])
    last.start()
    for copy in copies[1:] + [last]:
        copy.wait()


def shards(n_dp, n_ctx, inputs, block_order, w_value, query, keys, out_grad):
    x, q, k, g = inputs[0], query[0], keys[0], out_grad[0]
    rows, width = x.shape
    shard, hd = w_value.shape
    heads = q.shape[1] // hd
    group = 4 if heads % 4 == 0 else 1
    rounds = 0
    for turns in (1, 2):
        if shard % (16 * n_ctx * turns) == 0:
            rounds = turns
    pieces = max(rounds, 1) * (n_ctx if rounds else 1)
    part = shard // pieces
    chips = n_dp // 2
    copies = 2 * chips + max(chips, 1) + 8 + (chips - 1) * pieces + 4 * n_ctx
    hbm = pl.BlockSpec(memory_space=pltpu.HBM)
    o, dq, dk, fin = pl.pallas_call(
        functools.partial(kernel, n_dp, n_ctx, group, rounds),
        out_shape=(
            jax.ShapeDtypeStruct(q.shape, BF16),
            jax.ShapeDtypeStruct(q.shape, BF16),
            jax.ShapeDtypeStruct(k.shape, BF16),
            jax.ShapeDtypeStruct(w_value.shape, BF16),
        ),
        in_specs=[hbm] * 6,
        out_specs=(hbm,) * 4,
        scratch_shapes=[
            pltpu.VMEM(q.shape, BF16),
            pltpu.VMEM(q.shape, BF16),
            pltpu.VMEM(k.shape, BF16),
            pltpu.VMEM((shard, hd), BF16),
            pltpu.SMEM(block_order.shape, jnp.int32),
            pltpu.VMEM(q.shape, BF16),
            pltpu.VMEM(g.shape, BF16),
            pltpu.VMEM((2 * rows, width), BF16),
            pltpu.VMEM((width, hd), BF16),
            pltpu.VMEM((2 * rows, hd), BF16),
            pltpu.VMEM((2 * rows, hd), BF16),
            pltpu.VMEM((heads // group, 2 * rows, group * rows), F32),
            pltpu.VMEM((2 * rows, hd), F32),
            pltpu.VMEM((2 * rows, hd), F32),
            pltpu.VMEM((2, rows, hd), BF16),
            pltpu.VMEM((2, rows, hd), BF16),
            pltpu.VMEM((2 * rows, hd), BF16),
            pltpu.VMEM((width, hd), BF16),
            pltpu.VMEM((max(chips - 1, 1), shard, hd), BF16),
            pltpu.VMEM((shard, hd), BF16),
            pltpu.VMEM((max(rounds, 1), n_ctx, part, hd), BF16),
            pltpu.SemaphoreType.DMA((copies,)),
            pltpu.SemaphoreType.DMA((copies,)),
            pltpu.SemaphoreType.DMA((6,)),
        ],
        compiler_params=pltpu.CompilerParams(
            collective_id=0, has_side_effects=True, vmem_limit_bytes=60 * 2**20
        ),
    )(block_order, x, w_value, q, k, g)
    return pl.pallas_call(
        finish,
        out_shape=(
            jax.ShapeDtypeStruct(query.shape, BF16),
            jax.ShapeDtypeStruct(query.shape, BF16),
            jax.ShapeDtypeStruct(keys.shape, BF16),
            jax.ShapeDtypeStruct(w_value.shape, F32),
        ),
        in_specs=[hbm] * 4,
        out_specs=(hbm,) * 4,
        scratch_shapes=[
            pltpu.VMEM((shard, hd), BF16),
            pltpu.VMEM((shard, hd), F32),
            pltpu.SemaphoreType.DMA((5,)),
        ],
        compiler_params=pltpu.CompilerParams(vmem_limit_bytes=60 * 2**20),
    )(o[None], dq[None], dk[None], fin)


def solution(mesh):
    split = P("dp", "ctx", None)
    return jax.shard_map(
        functools.partial(shards, mesh.shape["dp"], mesh.shape["ctx"]),
        mesh=mesh,
        in_specs=(split, P(), P("dp", None), split, split, split),
        out_specs=(split, split, split, P("dp", None)),
        check_vma=False,
    )
```

```python
import functools

import jax
import jax.numpy as jnp
from jax import lax
from jax.experimental import pallas as pl
from jax.experimental.pallas import tpu as pltpu
from jax.sharding import PartitionSpec as P

MESH = pl.DeviceIdType.MESH
F32 = jnp.float32
BF16 = jnp.bfloat16


def mul16(value):
    return pl.multiple_of(value, 16)


def dot(a, b, ca, cb):
    return lax.dot_general(a, b, (((ca,), (cb,)), ((), ())), preferred_element_type=F32)


def chunk_of(width):
    best = 128
    for size in range(128, 1537, 128):
        if width % size == 0:
            best = size
    return best


def wide_of(chips):
    best = 1
    for size in range(1, chips + 1):
        if size * size <= chips and chips % size == 0:
            best = size
    return best


def kernel(
    n_dp, n_ctx, group, rounds,
    order_hbm, x, w, q_hbm, k, g_hbm,
    o_hbm, dq_hbm, dk_hbm, fin_hbm,
    o, dq, dk, fin, order, q, g, x2, w_all, k_all, v_all, probs, dv_acc, dk_acc, dvf, dkf, dv2, term, term_r, last_s, last_r, z_s, z_r,
    send_sem, recv_sem, local_sem,
):
    rows, width = x.shape
    shard, hd = w.shape
    heads = q.shape[1] // hd
    scale = 1.0 / hd**0.5
    chips = n_dp // 2
    pieces = max(rounds, 1) * (n_ctx if rounds else 1)
    part = shard // pieces
    aligned = shard % 128 == 0
    me = lax.axis_index("dp")
    z = lax.axis_index("ctx")
    chip, core = me // 2, lax.rem(me, 2)
    sib = me + 1 - 2 * core
    nxt = lax.rem(z + 1, n_ctx)
    prev = lax.rem(z + n_ctx - 1, n_ctx)

    wide = wide_of(chips)
    tall = chips // wide
    down, across = chip // wide, lax.rem(chip, wide)

    def device(i, j):
        return 2 * (lax.rem(down + tall + i, tall) * wide + lax.rem(across + wide + j, wide)) + core

    sides = [(0, j) for j in range(1, wide)]
    heights = [(i, 0) for i in range(1, tall)]
    others = [(i, j) for i in range(tall) for j in range(wide) if i or j]

    count = [0]
    sent = []

    def send(src, dst, target):
        at = count[0]
        count[0] += 1
        copy = pltpu.make_async_remote_copy(
            src_ref=src, dst_ref=dst, send_sem=send_sem.at[at], recv_sem=recv_sem.at[at],
            device_id=target, device_id_type=MESH,
        )
        copy.start()
        sent.append(copy)
        return at

    def arrived(ref, at):
        pltpu.make_async_remote_copy(
            src_ref=ref, dst_ref=ref, send_sem=send_sem.at[at], recv_sem=recv_sem.at[at],
            device_id={"dp": sib}, device_id_type=MESH,
        ).wait_recv()

    own = pl.ds(mul16(me * shard), shard)
    pairs = [
        (order_hbm, order), (k, k_all.at[pl.ds(0, rows)]), (q_hbm, q), (g_hbm, g),
        (x, x2.at[pl.ds(0, rows)]), (w, w_all.at[own]),
    ]
    loads = [
        pltpu.make_async_copy(src, dst, local_sem.at[i]) for i, (src, dst) in enumerate(pairs)
    ]
    for load in loads:
        load.start()

    barrier = pltpu.get_barrier_semaphore()
    near = sides + heights
    for i, j in near:
        pl.semaphore_signal(barrier, inc=1, device_id={"dp": device(i, j)}, device_id_type=MESH)
    pl.semaphore_signal(barrier, inc=1, device_id={"dp": sib}, device_id_type=MESH)
    for off in range(1, n_ctx):
        pl.semaphore_signal(
            barrier, inc=1, device_id={"ctx": lax.rem(z + off, n_ctx)}, device_id_type=MESH
        )
    pl.semaphore_wait(barrier, len(near) + n_ctx)

    keys_at = send(k, k_all.at[pl.ds(rows, rows)], {"ctx": nxt})
    half = shard // 2 if shard % 32 == 0 else shard
    halves = [(0, half, sides, heights)]
    if half < shard:
        halves.append((half, half, heights, sides))

    def w_rows(index, start, size):
        return w_all.at[pl.ds(mul16(index * shard + start), size)]

    w_at = {}

    def send_w(start, size, i, j, di, dj):
        src = w.at[pl.ds(start, size)] if not (i or j) else w_rows(device(-i, -j), start, size)
        dst = w_rows(device(-i, -j), start, size)
        w_at[start, i + di, j + dj] = send(src, dst, {"dp": device(di, dj)})

    for start, size, early, late in halves:
        for i, j in early:
            send_w(start, size, 0, 0, i, j)
    for start, size, early, late in halves:
        for i, j in late:
            send_w(start, size, 0, 0, i, j)
    w_sib_at = {}
    for start, size, early, late in halves:
        src = w.at[pl.ds(start, size)]
        w_sib_at[start, 0, 0] = send(src, w_rows(me, start, size), {"dp": sib})
    x_at = []
    if aligned:
        for j in range(chips):
            cols = pl.ds(pl.multiple_of((2 * j + 1 - core) * shard, 128), shard)
            x_at.append(send(x.at[:, cols], x2.at[pl.ds(rows, rows), cols], {"dp": sib}))
    else:
        x_at.append(send(x, x2.at[pl.ds(rows, rows)], {"dp": sib}))
    loads[0].wait()

    per = order.shape[0] // n_ctx
    blk = rows // per
    span = group * rows
    key_row = lax.broadcasted_iota(jnp.int32, (2 * rows, span), 0)
    q_col = lax.rem(lax.broadcasted_iota(jnp.int32, (2 * rows, span), 1), rows)
    key_place = jnp.zeros((2 * rows, span), jnp.int32)
    q_place = jnp.zeros((2 * rows, span), jnp.int32)
    for b in range(per):
        mine = order[z * per + b]
        theirs = order[prev * per + b]
        key_place = jnp.where(key_row // blk == b, mine * blk + key_row - b * blk, key_place)
        key_place = jnp.where(
            key_row // blk == per + b, theirs * blk + key_row - (per + b) * blk, key_place
        )
        q_place = jnp.where(q_col // blk == b, mine * blk + q_col - b * blk, q_place)
    bias = jnp.where(key_place <= q_place, 0.0, -1e30).astype(F32)

    def stacked(ref, it):
        return jnp.concatenate(
            [
                ref[:, pl.ds(pl.multiple_of((it * group + i) * hd, 128), hd)]
                for i in range(group)
            ],
            axis=0,
        )

    for load in loads[1:4]:
        load.wait()
    arrived(k_all.at[pl.ds(rows, rows)], keys_at)
    dv_acc[...] = jnp.zeros_like(dv_acc)
    dk_acc[...] = jnp.zeros_like(dk_acc)

    def first(it, carry):
        scores = dot(k_all[...], stacked(q, it), 1, 1) * scale
        scores = jnp.where(bias < 0.0, -1e30, scores)
        top = jnp.max(scores, axis=0, keepdims=True)
        weights = jnp.exp(scores - top)
        prob = weights * (1.0 / jnp.sum(weights, axis=0, keepdims=True))
        probs[it] = prob
        dv_acc[...] += dot(prob.astype(BF16), stacked(g, it), 1, 0)
        return carry

    lax.fori_loop(0, heads // group, first, 0)

    def w_came(start, size, i, j):
        came = w_rows(device(-i, -j), start, size)
        arrived(came, w_at[start, i, j])
        w_sib_at[start, i, j] = send(came, came, {"dp": sib})

    dvf[0] = dv_acc[pl.ds(rows, rows)].astype(BF16)
    at = send(dvf.at[0], dvf.at[1], {"ctx": prev})
    for start, size, early, late in halves:
        for i, j in early:
            arrived(w_rows(device(-i, -j), start, size), w_at[start, i, j])
            for di, dj in late:
                send_w(start, size, i, j, di, dj)
            came = w_rows(device(-i, -j), start, size)
            w_sib_at[start, i, j] = send(came, came, {"dp": sib})
    loads[4].wait()
    arrived(dvf.at[1], at)
    dv2[pl.ds(0, rows)] = (dv_acc[pl.ds(0, rows)] + dvf[1].astype(F32)).astype(BF16)
    at = send(dv2.at[pl.ds(0, rows)], dv2.at[pl.ds(rows, rows)], {"dp": sib})
    for j in range(len(x_at)):
        if aligned:
            cols = pl.ds(pl.multiple_of((2 * j + core) * shard, 128), shard)
            arrived(x2.at[pl.ds(rows, rows), cols], x_at[j])
        else:
            arrived(x2.at[pl.ds(rows, rows)], x_at[j])
    arrived(dv2.at[pl.ds(rows, rows)], at)

    def shard_term(index):
        cols = pl.ds(pl.multiple_of(index * shard, 128), shard)
        term[pl.ds(mul16(index * shard), shard)] = dot(x2[:, cols], dv2[...], 0, 0).astype(BF16)

    if aligned:
        for i, j in others:
            shard_term(device(i, j))
    else:
        size = chunk_of(width)
        for start in range(0, width, size):
            cols = pl.ds(start, size)
            term[cols] = dot(x2[:, cols], dv2[...], 0, 0).astype(BF16)
    def piece(index):
        if not rounds:
            return 0
        return (index // n_ctx) * n_ctx + lax.rem(z + 1 + index % n_ctx, n_ctx)

    def piece_rows(index):
        return pl.ds(mul16(piece(index) * part), part)

    def lanes(index):
        return (sides, heights) if index % 2 == 0 else (heights, sides)

    def term_rows(index, i, j):
        return term.at[pl.ds(mul16(device(i, j) * shard + piece(index) * part), part)]

    term_at = []
    for index in range(pieces):
        early, late = lanes(index)
        there = piece_rows(index)
        line = {}
        for n, (i, j) in enumerate(late + [(0, 0)]):
            for m, (di, dj) in enumerate(early):
                line[n, m] = send(
                    term_rows(index, i + di, j + dj), term_r.at[m, n, there], {"dp": device(di, dj)}
                )
        term_at.append(line)
    if aligned:
        shard_term(me)

    last_at = []

    def pass_piece(index):
        early, late = lanes(index)
        there = piece_rows(index)
        line = []
        for n, (i, j) in enumerate(late):
            total = term_rows(index, i, j)[...].astype(F32)
            for m in range(len(early)):
                arrived(term_r.at[m, n, there], term_at[index][n, m])
                total += term_r[m, n, there].astype(F32)
            last_s[n, there] = total.astype(BF16)
            line.append(send(last_s.at[n, there], last_r.at[n, there], {"dp": device(i, j)}))
        last_at.append(line)

    loads[5].wait()
    for start, size, early, late in halves:
        for i, j in late:
            w_came(start, size, i, j)
        for i, j in others:
            if i and j:
                w_came(start, size, i, j)
    pass_piece(0)
    if pieces > 1:
        pass_piece(1)
    for start, size, early, late in halves:
        for i, j in [(0, 0)] + others:
            arrived(w_rows(device(-i, -j) + 1 - 2 * core, start, size), w_sib_at[start, i, j])
    v_own = pl.ds(0, rows)
    v_far = pl.ds(rows, rows)
    size = chunk_of(width)

    def project(it, total):
        cols = pl.ds(pl.multiple_of(it * size, 128), size)
        return total + dot(x2[pl.ds(0, rows), cols], w_all[cols], 1, 0)

    total = lax.fori_loop(0, width // size, project, jnp.zeros((rows, hd), F32))
    v_all[v_own] = total.astype(BF16)
    at = send(v_all.at[v_own], v_all.at[v_far], {"ctx": nxt})

    z_at = []

    def finish_piece(index):
        there = piece_rows(index)
        total = term[pl.ds(mul16(me * shard + piece(index) * part), part)].astype(F32)
        early, late = lanes(index)
        for m in range(len(early)):
            arrived(term_r.at[m, len(late), there], term_at[index][len(late), m])
            total += term_r[m, len(late), there].astype(F32)
        for n in range(len(late)):
            arrived(last_r.at[n, there], last_at[index][n])
            total += last_r[n, there].astype(F32)
        if not rounds:
            z_s[...] = total.astype(BF16)
            z_r[0, z] = z_s[...]
            for off in range(1, n_ctx):
                z_at.append(send(z_s, z_r.at[0, z], {"ctx": lax.rem(z + off, n_ctx)}))
            return
        turn, step = index // n_ctx, index % n_ctx
        if step < n_ctx - 1:
            z_s[there] = total.astype(BF16)
            target = {"ctx": lax.rem(z + 1 + step, n_ctx)}
            z_at.append(send(z_s.at[there], z_r.at[turn, z], target))
        else:
            z_r[turn, z] = total.astype(BF16)

    f_at = []

    def finish_round(turn):
        for off in range(1, n_ctx):
            at = z_at[turn * (n_ctx - 1) + off - 1]
            arrived(z_r.at[turn, lax.rem(z + n_ctx - off, n_ctx)], at)
        total = z_r[turn, 0].astype(F32)
        for index in range(1, n_ctx):
            total += z_r[turn, index].astype(F32)
        if not rounds:
            fin[...] = total.astype(BF16)
            return
        mine = pl.ds(mul16((turn * n_ctx + z) * part), part)
        fin[mine] = total.astype(BF16)
        for off in range(1, n_ctx):
            f_at.append(send(fin.at[mine], fin.at[mine], {"ctx": lax.rem(z + off, n_ctx)}))

    for index in range(2, min(4, pieces)):
        pass_piece(index)
    arrived(v_all.at[v_far], at)
    v_t = v_all[...].T
    k_t = k_all[...].T

    def second(it, carry):
        prob = probs[it]
        q_rows = stacked(q, it)
        out_t = dot(v_t, prob.astype(BF16), 1, 0)
        dprob = dot(v_all[...], stacked(g, it), 1, 1)
        delta = jnp.sum(prob * dprob, axis=0, keepdims=True)
        dscore = (prob * (dprob - delta)).astype(BF16)
        dk_acc[...] += dot(dscore, q_rows, 1, 0)
        dq_t = dot(k_t, dscore, 1, 0) * scale
        for i in range(group):
            cols = pl.ds(pl.multiple_of((it * group + i) * hd, 128), hd)
            o[:, cols] = out_t[:, i * rows:(i + 1) * rows].T.astype(BF16)
            dq[:, cols] = dq_t[:, i * rows:(i + 1) * rows].T.astype(BF16)
        return carry

    steps = heads // group
    jobs = []
    for index in range(pieces):
        if index + 4 < pieces:
            jobs.append(functools.partial(pass_piece, index + 4))
        jobs.append(functools.partial(finish_piece, index))
        if index + 1 == n_ctx and rounds:
            jobs.append(functools.partial(finish_round, 0))
    done = 0
    for it in range(steps):
        second(it, 0)
        upto = 2 * (it + 1) if it + 1 < steps else min(8, len(jobs))
        for job in jobs[done:upto]:
            job()
        done = min(upto, len(jobs))
    stores = [
        pltpu.make_async_copy(src, dst, local_sem.at[i])
        for i, (src, dst) in enumerate([(o, o_hbm), (dq, dq_hbm), (dk, dk_hbm), (fin, fin_hbm)])
    ]
    stores[0].start()
    stores[1].start()
    dkf[0] = (dk_acc[pl.ds(rows, rows)] * scale).astype(BF16)
    dk_at = send(dkf.at[0], dkf.at[1], {"ctx": prev})
    for job in jobs[done:]:
        job()
    if not rounds:
        finish_round(0)
    arrived(dkf.at[1], dk_at)
    dk[...] = (dk_acc[pl.ds(0, rows)] * scale + dkf[1].astype(F32)).astype(BF16)
    stores[2].start()
    for turn in range(1, rounds):
        finish_round(turn)
    for turn in range(rounds):
        for off in range(1, n_ctx):
            index = turn * n_ctx + lax.rem(z + n_ctx - off, n_ctx)
            theirs = pl.ds(mul16(index * part), part)
            arrived(fin.at[theirs], f_at[turn * (n_ctx - 1) + off - 1])
    stores[3].start()
    for copy in sent:
        copy.wait_send()
    for copy in stores:
        copy.wait()


def finish(o, dq, dk, fin, o_out, dq_out, dk_out, gw, o_v, dq_v, dk_v, narrow, wide, sem):
    ins = [(fin, narrow), (o, o_v), (dq, dq_v), (dk, dk_v)]
    outs = [(wide, gw), (o_v, o_out), (dq_v, dq_out), (dk_v, dk_out)]
    loads = [pltpu.make_async_copy(src, dst, sem.at[i]) for i, (src, dst) in enumerate(ins)]
    stores = [pltpu.make_async_copy(src, dst, sem.at[4 + i]) for i, (src, dst) in enumerate(outs)]
    for load in loads:
        load.start()
    for index in range(4):
        loads[index].wait()
        if index == 0:
            wide[...] = narrow[...].astype(F32)
        stores[index].start()
    for store in stores:
        store.wait()


def shards(n_dp, n_ctx, inputs, block_order, w_value, query, keys, out_grad):
    x, q, k, g = inputs[0], query[0], keys[0], out_grad[0]
    rows, width = x.shape
    shard, hd = w_value.shape
    heads = q.shape[1] // hd
    group = 4 if heads % 4 == 0 else 1
    rounds = 0
    for turns in (1, 2):
        if shard % (16 * n_ctx * turns) == 0:
            rounds = turns
    pieces = max(rounds, 1) * (n_ctx if rounds else 1)
    part = shard // pieces
    chips = n_dp // 2
    most = chips // wide_of(chips)
    copies = 5 * chips + 16 + 2 * chips * pieces + 4 * n_ctx
    hbm = pl.BlockSpec(memory_space=pltpu.HBM)
    o, dq, dk, fin = pl.pallas_call(
        functools.partial(kernel, n_dp, n_ctx, group, rounds),
        out_shape=(
            jax.ShapeDtypeStruct(q.shape, BF16),
            jax.ShapeDtypeStruct(q.shape, BF16),
            jax.ShapeDtypeStruct(k.shape, BF16),
            jax.ShapeDtypeStruct(w_value.shape, BF16),
        ),
        in_specs=[hbm] * 6,
        out_specs=(hbm,) * 4,
        scratch_shapes=[
            pltpu.VMEM(q.shape, BF16),
            pltpu.VMEM(q.shape, BF16),
            pltpu.VMEM(k.shape, BF16),
            pltpu.VMEM((shard, hd), BF16),
            pltpu.SMEM(block_order.shape, jnp.int32),
            pltpu.VMEM(q.shape, BF16),
            pltpu.VMEM(g.shape, BF16),
            pltpu.VMEM((2 * rows, width), BF16),
            pltpu.VMEM((width, hd), BF16),
            pltpu.VMEM((2 * rows, hd), BF16),
            pltpu.VMEM((2 * rows, hd), BF16),
            pltpu.VMEM((heads // group, 2 * rows, group * rows), F32),
            pltpu.VMEM((2 * rows, hd), F32),
            pltpu.VMEM((2 * rows, hd), F32),
            pltpu.VMEM((2, rows, hd), BF16),
            pltpu.VMEM((2, rows, hd), BF16),
            pltpu.VMEM((2 * rows, hd), BF16),
            pltpu.VMEM((width, hd), BF16),
            pltpu.VMEM((most, most, shard, hd), BF16),
            pltpu.VMEM((most, shard, hd), BF16),
            pltpu.VMEM((most, shard, hd), BF16),
            pltpu.VMEM((shard, hd), BF16),
            pltpu.VMEM((max(rounds, 1), n_ctx, part, hd), BF16),
            pltpu.SemaphoreType.DMA((copies,)),
            pltpu.SemaphoreType.DMA((copies,)),
            pltpu.SemaphoreType.DMA((6,)),
        ],
        compiler_params=pltpu.CompilerParams(
            collective_id=0, has_side_effects=True, vmem_limit_bytes=60 * 2**20
        ),
    )(block_order, x, w_value, q, k, g)
    return pl.pallas_call(
        finish,
        out_shape=(
            jax.ShapeDtypeStruct(query.shape, BF16),
            jax.ShapeDtypeStruct(query.shape, BF16),
            jax.ShapeDtypeStruct(keys.shape, BF16),
            jax.ShapeDtypeStruct(w_value.shape, F32),
        ),
        in_specs=[hbm] * 4,
        out_specs=(hbm,) * 4,
        scratch_shapes=[
            pltpu.VMEM(query.shape, BF16),
            pltpu.VMEM(query.shape, BF16),
            pltpu.VMEM(keys.shape, BF16),
            pltpu.VMEM((shard, hd), BF16),
            pltpu.VMEM((shard, hd), F32),
            pltpu.SemaphoreType.DMA((8,)),
        ],
        compiler_params=pltpu.CompilerParams(vmem_limit_bytes=60 * 2**20),
    )(o[None], dq[None], dk[None], fin)


def solution(mesh):
    split = P("dp", "ctx", None)
    return jax.shard_map(
        functools.partial(shards, mesh.shape["dp"], mesh.shape["ctx"]),
        mesh=mesh,
        in_specs=(split, P(), P("dp", None), split, split, split),
        out_specs=(split, split, split, P("dp", None)),
        check_vma=False,
    )
```

```python
import functools

import jax
import jax.numpy as jnp
from jax import lax
from jax.experimental import pallas as pl
from jax.experimental.pallas import tpu as pltpu
from jax.sharding import PartitionSpec as P

MESH = pl.DeviceIdType.MESH
F32 = jnp.float32
BF16 = jnp.bfloat16


def mul16(value):
    return pl.multiple_of(value, 16)


def dot(a, b, ca, cb):
    return lax.dot_general(a, b, (((ca,), (cb,)), ((), ())), preferred_element_type=F32)


def chunk_of(width):
    best = 128
    for size in range(128, 1537, 128):
        if width % size == 0:
            best = size
    return best


def wide_of(chips):
    best = 1
    for size in range(1, chips + 1):
        if size * size <= chips and chips % size == 0:
            best = size
    return best


def kernel(
    n_dp, n_ctx, group, rounds,
    order_hbm, x, w, q_hbm, k, g_hbm,
    o_hbm, dq_hbm, dk_hbm, fin_hbm,
    o, dq, dk, fin, order, q, g, x2, w_all, k_all, v_all, probs, dv_acc, dk_acc, dvf, dkf, dv2, term, term_r, last_s, last_r, z_s, z_r,
    send_sem, recv_sem, local_sem,
):
    rows, width = x.shape
    shard, hd = w.shape
    heads = q.shape[1] // hd
    scale = 1.0 / hd**0.5
    chips = n_dp // 2
    pieces = max(rounds, 1) * (n_ctx if rounds else 1)
    part = shard // pieces
    aligned = shard % 128 == 0
    me = lax.axis_index("dp")
    z = lax.axis_index("ctx")
    chip, core = me // 2, lax.rem(me, 2)
    sib = me + 1 - 2 * core
    nxt = lax.rem(z + 1, n_ctx)
    prev = lax.rem(z + n_ctx - 1, n_ctx)

    wide = wide_of(chips)
    tall = chips // wide
    down, across = chip // wide, lax.rem(chip, wide)

    def device(i, j):
        return 2 * (lax.rem(down + tall + i, tall) * wide + lax.rem(across + wide + j, wide)) + core

    sides = [(0, j) for j in range(1, wide)]
    heights = [(i, 0) for i in range(1, tall)]
    others = [(i, j) for i in range(tall) for j in range(wide) if i or j]

    count = [0]
    sent = []

    def send(src, dst, target):
        at = count[0]
        count[0] += 1
        copy = pltpu.make_async_remote_copy(
            src_ref=src, dst_ref=dst, send_sem=send_sem.at[at], recv_sem=recv_sem.at[at],
            device_id=target, device_id_type=MESH,
        )
        copy.start()
        sent.append(copy)
        return at

    def arrived(ref, at):
        pltpu.make_async_remote_copy(
            src_ref=ref, dst_ref=ref, send_sem=send_sem.at[at], recv_sem=recv_sem.at[at],
            device_id={"dp": sib}, device_id_type=MESH,
        ).wait_recv()

    own = pl.ds(mul16(me * shard), shard)
    pairs = [
        (order_hbm, order), (k, k_all.at[pl.ds(0, rows)]), (q_hbm, q), (g_hbm, g),
        (x, x2.at[pl.ds(0, rows)]), (w, w_all.at[own]),
    ]
    loads = [
        pltpu.make_async_copy(src, dst, local_sem.at[i]) for i, (src, dst) in enumerate(pairs)
    ]
    for load in loads:
        load.start()

    barrier = pltpu.get_barrier_semaphore()
    near = sides + heights
    for i, j in near:
        pl.semaphore_signal(barrier, inc=1, device_id={"dp": device(i, j)}, device_id_type=MESH)
    pl.semaphore_signal(barrier, inc=1, device_id={"dp": sib}, device_id_type=MESH)
    for off in range(1, n_ctx):
        pl.semaphore_signal(
            barrier, inc=1, device_id={"ctx": lax.rem(z + off, n_ctx)}, device_id_type=MESH
        )
    pl.semaphore_wait(barrier, len(near) + n_ctx)

    keys_at = send(k, k_all.at[pl.ds(rows, rows)], {"ctx": nxt})
    half = shard // 2 if shard % 32 == 0 else shard
    halves = [(0, half, sides, heights)]
    if half < shard:
        halves.append((half, half, heights, sides))

    def w_rows(index, start, size):
        return w_all.at[pl.ds(mul16(index * shard + start), size)]

    w_at = {}

    def send_w(start, size, i, j, di, dj):
        src = w.at[pl.ds(start, size)] if not (i or j) else w_rows(device(-i, -j), start, size)
        dst = w_rows(device(-i, -j), start, size)
        w_at[start, i + di, j + dj] = send(src, dst, {"dp": device(di, dj)})

    for start, size, early, late in halves:
        for i, j in early:
            send_w(start, size, 0, 0, i, j)
    for start, size, early, late in halves:
        for i, j in late:
            send_w(start, size, 0, 0, i, j)
    w_sib_at = {}
    for start, size, early, late in halves:
        src = w.at[pl.ds(start, size)]
        w_sib_at[start, 0, 0] = send(src, w_rows(me, start, size), {"dp": sib})
    x_at = []
    if aligned:
        for j in range(chips):
            cols = pl.ds(pl.multiple_of((2 * j + 1 - core) * shard, 128), shard)
            x_at.append(send(x.at[:, cols], x2.at[pl.ds(rows, rows), cols], {"dp": sib}))
    else:
        x_at.append(send(x, x2.at[pl.ds(rows, rows)], {"dp": sib}))
    loads[0].wait()

    per = order.shape[0] // n_ctx
    blk = rows // per
    key_row = lax.broadcasted_iota(jnp.int32, (2 * rows, rows), 0)
    q_row = lax.broadcasted_iota(jnp.int32, (2 * rows, rows), 1)
    key_place = key_row
    q_place = q_row
    for b in range(per):
        mine = order[z * per + b]
        q_place = jnp.where(q_row >= b * blk, q_row + (mine - b) * blk, q_place)
    for b in range(2 * per):
        owner = z if b < per else prev
        block = order[owner * per + b % per]
        key_place = jnp.where(key_row >= b * blk, key_row + (block - b) * blk, key_place)
    hidden = jnp.where(key_place <= q_place, 0.0, 1.0).astype(F32)
    hidden = jnp.concatenate([hidden] * group, axis=1)

    def stacked(ref, it):
        return jnp.concatenate(
            [
                ref[:, pl.ds((it * group + i) * hd, hd)]
                for i in range(group)
            ],
            axis=0,
        )

    for load in loads[1:4]:
        load.wait()
    arrived(k_all.at[pl.ds(rows, rows)], keys_at)
    dv_acc[...] = jnp.zeros_like(dv_acc)
    dk_acc[...] = jnp.zeros_like(dk_acc)

    def first(it, carry):
        scores = dot(k_all[...], stacked(q, it), 1, 1) * scale
        scores = jnp.where(hidden > 0.0, -1e30, scores)
        top = jnp.max(scores, axis=0, keepdims=True)
        weights = jnp.exp(scores - top)
        prob = weights * (1.0 / jnp.sum(weights, axis=0, keepdims=True))
        probs[it] = prob
        dv_acc[...] += dot(prob.astype(BF16), stacked(g, it), 1, 0)
        return carry

    for it in range(heads // group):
        first(it, 0)

    def w_came(start, size, i, j):
        came = w_rows(device(-i, -j), start, size)
        arrived(came, w_at[start, i, j])
        w_sib_at[start, i, j] = send(came, came, {"dp": sib})

    dvf[0] = dv_acc[pl.ds(rows, rows)].astype(BF16)
    at = send(dvf.at[0], dvf.at[1], {"ctx": prev})
    for start, size, early, late in halves:
        for i, j in early:
            arrived(w_rows(device(-i, -j), start, size), w_at[start, i, j])
            for di, dj in late:
                send_w(start, size, i, j, di, dj)
            came = w_rows(device(-i, -j), start, size)
            w_sib_at[start, i, j] = send(came, came, {"dp": sib})
    loads[4].wait()
    arrived(dvf.at[1], at)
    dv2[pl.ds(0, rows)] = (dv_acc[pl.ds(0, rows)] + dvf[1].astype(F32)).astype(BF16)
    at = send(dv2.at[pl.ds(0, rows)], dv2.at[pl.ds(rows, rows)], {"dp": sib})
    for j in range(len(x_at)):
        if aligned:
            cols = pl.ds(pl.multiple_of((2 * j + core) * shard, 128), shard)
            arrived(x2.at[pl.ds(rows, rows), cols], x_at[j])
        else:
            arrived(x2.at[pl.ds(rows, rows)], x_at[j])
    arrived(dv2.at[pl.ds(rows, rows)], at)

    def shard_term(index):
        cols = pl.ds(pl.multiple_of(index * shard, 128), shard)
        term[pl.ds(mul16(index * shard), shard)] = dot(x2[:, cols], dv2[...], 0, 0).astype(BF16)

    if aligned:
        for i, j in others:
            shard_term(device(i, j))
    else:
        size = chunk_of(width)
        for start in range(0, width, size):
            cols = pl.ds(start, size)
            term[cols] = dot(x2[:, cols], dv2[...], 0, 0).astype(BF16)
    def piece(index):
        if not rounds:
            return 0
        return (index // n_ctx) * n_ctx + lax.rem(z + 1 + index % n_ctx, n_ctx)

    def piece_rows(index):
        return pl.ds(mul16(piece(index) * part), part)

    def lanes(index):
        return (sides, heights) if index % 2 == 0 else (heights, sides)

    def term_rows(index, i, j):
        return term.at[pl.ds(mul16(device(i, j) * shard + piece(index) * part), part)]

    term_at = []
    for index in range(pieces):
        early, late = lanes(index)
        there = piece_rows(index)
        line = {}
        for n, (i, j) in enumerate(late + [(0, 0)]):
            for m, (di, dj) in enumerate(early):
                line[n, m] = send(
                    term_rows(index, i + di, j + dj), term_r.at[m, n, there], {"dp": device(di, dj)}
                )
        term_at.append(line)

    last_at = []

    def pass_piece(index):
        early, late = lanes(index)
        there = piece_rows(index)
        line = []
        for n, (i, j) in enumerate(late):
            total = term_rows(index, i, j)[...].astype(F32)
            for m in range(len(early)):
                arrived(term_r.at[m, n, there], term_at[index][n, m])
                total += term_r[m, n, there].astype(F32)
            last_s[n, there] = total.astype(BF16)
            line.append(send(last_s.at[n, there], last_r.at[n, there], {"dp": device(i, j)}))
        last_at.append(line)

    loads[5].wait()
    for start, size, early, late in halves:
        for i, j in late:
            w_came(start, size, i, j)
        for i, j in others:
            if i and j:
                w_came(start, size, i, j)
    for start, size, early, late in halves:
        for i, j in [(0, 0)] + others:
            arrived(w_rows(device(-i, -j) + 1 - 2 * core, start, size), w_sib_at[start, i, j])
    v_own = pl.ds(0, rows)
    v_far = pl.ds(rows, rows)
    size = chunk_of(width)

    total = jnp.zeros((rows, hd), F32)
    for start in range(0, width, size):
        cols = pl.ds(start, size)
        total = total + dot(x2[pl.ds(0, rows), cols], w_all[cols], 1, 0)
    v_all[v_own] = total.astype(BF16)
    at = send(v_all.at[v_own], v_all.at[v_far], {"ctx": nxt})

    z_at = []

    def finish_piece(index):
        there = piece_rows(index)
        total = term[pl.ds(mul16(me * shard + piece(index) * part), part)].astype(F32)
        early, late = lanes(index)
        for m in range(len(early)):
            arrived(term_r.at[m, len(late), there], term_at[index][len(late), m])
            total += term_r[m, len(late), there].astype(F32)
        for n in range(len(late)):
            arrived(last_r.at[n, there], last_at[index][n])
            total += last_r[n, there].astype(F32)
        if not rounds:
            z_s[...] = total.astype(BF16)
            z_r[0, z] = z_s[...]
            for off in range(1, n_ctx):
                z_at.append(send(z_s, z_r.at[0, z], {"ctx": lax.rem(z + off, n_ctx)}))
            return
        turn, step = index // n_ctx, index % n_ctx
        if step < n_ctx - 1:
            z_s[there] = total.astype(BF16)
            target = {"ctx": lax.rem(z + 1 + step, n_ctx)}
            z_at.append(send(z_s.at[there], z_r.at[turn, z], target))
        else:
            z_r[turn, z] = total.astype(BF16)

    f_at = []

    def finish_round(turn):
        for off in range(1, n_ctx):
            at = z_at[turn * (n_ctx - 1) + off - 1]
            arrived(z_r.at[turn, lax.rem(z + n_ctx - off, n_ctx)], at)
        total = z_r[turn, 0].astype(F32)
        for index in range(1, n_ctx):
            total += z_r[turn, index].astype(F32)
        if not rounds:
            fin[...] = total.astype(BF16)
            return
        mine = pl.ds(mul16((turn * n_ctx + z) * part), part)
        fin[mine] = total.astype(BF16)
        for off in range(1, n_ctx):
            f_at.append(send(fin.at[mine], fin.at[mine], {"ctx": lax.rem(z + off, n_ctx)}))

    if aligned:
        shard_term(me)
    for index in range(min(4, pieces)):
        pass_piece(index)
    arrived(v_all.at[v_far], at)
    v_t = v_all[...].T
    k_t = k_all[...].T

    def second(it, carry):
        prob = probs[it]
        q_rows = stacked(q, it)
        out_t = dot(v_t, prob.astype(BF16), 1, 0)
        dprob = dot(v_all[...], stacked(g, it), 1, 1)
        delta = jnp.sum(prob * dprob, axis=0, keepdims=True)
        dscore = (prob * (dprob - delta)).astype(BF16)
        dk_acc[...] += dot(dscore, q_rows, 1, 0)
        dq_t = dot(k_t, dscore, 1, 0) * scale
        for i in range(group):
            cols = pl.ds((it * group + i) * hd, hd)
            o[:, cols] = out_t[:, i * rows:(i + 1) * rows].astype(BF16).T
            dq[:, cols] = dq_t[:, i * rows:(i + 1) * rows].astype(BF16).T
        return carry

    steps = heads // group
    jobs = []
    for index in range(pieces):
        if index + 4 < pieces:
            jobs.append(functools.partial(pass_piece, index + 4))
        jobs.append(functools.partial(finish_piece, index))
        if index + 1 == n_ctx and rounds:
            jobs.append(functools.partial(finish_round, 0))
    done = 0
    for it in range(steps):
        second(it, 0)
        upto = 2 * (it + 1) if it + 1 < steps else min(8, len(jobs))
        for job in jobs[done:upto]:
            job()
        done = min(upto, len(jobs))
    stores = [
        pltpu.make_async_copy(src, dst, local_sem.at[i])
        for i, (src, dst) in enumerate([(o, o_hbm), (dq, dq_hbm), (dk, dk_hbm), (fin, fin_hbm)])
    ]
    stores[0].start()
    stores[1].start()
    dkf[0] = (dk_acc[pl.ds(rows, rows)] * scale).astype(BF16)
    dk_at = send(dkf.at[0], dkf.at[1], {"ctx": prev})
    for job in jobs[done:]:
        job()
    if not rounds:
        finish_round(0)
    arrived(dkf.at[1], dk_at)
    dk[...] = (dk_acc[pl.ds(0, rows)] * scale + dkf[1].astype(F32)).astype(BF16)
    stores[2].start()
    for turn in range(1, rounds):
        finish_round(turn)
    for turn in range(rounds):
        for off in range(1, n_ctx):
            index = turn * n_ctx + lax.rem(z + n_ctx - off, n_ctx)
            theirs = pl.ds(mul16(index * part), part)
            arrived(fin.at[theirs], f_at[turn * (n_ctx - 1) + off - 1])
    stores[3].start()
    for copy in sent:
        copy.wait_send()
    for copy in stores:
        copy.wait()


def finish(o, dq, dk, fin, o_out, dq_out, dk_out, gw, o_v, dq_v, dk_v, narrow, wide, sem):
    ins = [(fin, narrow), (o, o_v), (dq, dq_v), (dk, dk_v)]
    outs = [(wide, gw), (o_v, o_out), (dq_v, dq_out), (dk_v, dk_out)]
    loads = [pltpu.make_async_copy(src, dst, sem.at[i]) for i, (src, dst) in enumerate(ins)]
    stores = [pltpu.make_async_copy(src, dst, sem.at[4 + i]) for i, (src, dst) in enumerate(outs)]
    for load in loads:
        load.start()
    for index in range(4):
        loads[index].wait()
        if index == 0:
            wide[...] = narrow[...].astype(F32)
        stores[index].start()
    for store in stores:
        store.wait()


def shards(n_dp, n_ctx, inputs, block_order, w_value, query, keys, out_grad):
    x, q, k, g = inputs[0], query[0], keys[0], out_grad[0]
    rows, width = x.shape
    shard, hd = w_value.shape
    heads = q.shape[1] // hd
    group = 4 if heads % 4 == 0 else 1
    rounds = 0
    for turns in (1, 2):
        if shard % (16 * n_ctx * turns) == 0:
            rounds = turns
    pieces = max(rounds, 1) * (n_ctx if rounds else 1)
    part = shard // pieces
    chips = n_dp // 2
    most = chips // wide_of(chips)
    copies = 5 * chips + 16 + 2 * chips * pieces + 4 * n_ctx
    hbm = pl.BlockSpec(memory_space=pltpu.HBM)
    o, dq, dk, fin = pl.pallas_call(
        functools.partial(kernel, n_dp, n_ctx, group, rounds),
        out_shape=(
            jax.ShapeDtypeStruct(q.shape, BF16),
            jax.ShapeDtypeStruct(q.shape, BF16),
            jax.ShapeDtypeStruct(k.shape, BF16),
            jax.ShapeDtypeStruct(w_value.shape, BF16),
        ),
        in_specs=[hbm] * 6,
        out_specs=(hbm,) * 4,
        scratch_shapes=[
            pltpu.VMEM(q.shape, BF16),
            pltpu.VMEM(q.shape, BF16),
            pltpu.VMEM(k.shape, BF16),
            pltpu.VMEM((shard, hd), BF16),
            pltpu.SMEM(block_order.shape, jnp.int32),
            pltpu.VMEM(q.shape, BF16),
            pltpu.VMEM(g.shape, BF16),
            pltpu.VMEM((2 * rows, width), BF16),
            pltpu.VMEM((width, hd), BF16),
            pltpu.VMEM((2 * rows, hd), BF16),
            pltpu.VMEM((2 * rows, hd), BF16),
            pltpu.VMEM((heads // group, 2 * rows, group * rows), F32),
            pltpu.VMEM((2 * rows, hd), F32),
            pltpu.VMEM((2 * rows, hd), F32),
            pltpu.VMEM((2, rows, hd), BF16),
            pltpu.VMEM((2, rows, hd), BF16),
            pltpu.VMEM((2 * rows, hd), BF16),
            pltpu.VMEM((width, hd), BF16),
            pltpu.VMEM((most, most, shard, hd), BF16),
            pltpu.VMEM((most, shard, hd), BF16),
            pltpu.VMEM((most, shard, hd), BF16),
            pltpu.VMEM((shard, hd), BF16),
            pltpu.VMEM((max(rounds, 1), n_ctx, part, hd), BF16),
            pltpu.SemaphoreType.DMA((copies,)),
            pltpu.SemaphoreType.DMA((copies,)),
            pltpu.SemaphoreType.DMA((6,)),
        ],
        compiler_params=pltpu.CompilerParams(
            collective_id=0, has_side_effects=True, vmem_limit_bytes=60 * 2**20
        ),
    )(block_order, x, w_value, q, k, g)
    return pl.pallas_call(
        finish,
        out_shape=(
            jax.ShapeDtypeStruct(query.shape, BF16),
            jax.ShapeDtypeStruct(query.shape, BF16),
            jax.ShapeDtypeStruct(keys.shape, BF16),
            jax.ShapeDtypeStruct(w_value.shape, F32),
        ),
        in_specs=[hbm] * 4,
        out_specs=(hbm,) * 4,
        scratch_shapes=[
            pltpu.VMEM(query.shape, BF16),
            pltpu.VMEM(query.shape, BF16),
            pltpu.VMEM(keys.shape, BF16),
            pltpu.VMEM((shard, hd), BF16),
            pltpu.VMEM((shard, hd), F32),
            pltpu.SemaphoreType.DMA((8,)),
        ],
        compiler_params=pltpu.CompilerParams(vmem_limit_bytes=60 * 2**20),
    )(o[None], dq[None], dk[None], fin)


def solution(mesh):
    split = P("dp", "ctx", None)
    return jax.shard_map(
        functools.partial(shards, mesh.shape["dp"], mesh.shape["ctx"]),
        mesh=mesh,
        in_specs=(split, P(), P("dp", None), split, split, split),
        out_specs=(split, split, split, P("dp", None)),
        check_vma=False,
    )
```

```python
import functools

import jax
import jax.numpy as jnp
from jax import lax
from jax.experimental import pallas as pl
from jax.experimental.pallas import tpu as pltpu
from jax.sharding import PartitionSpec as P

MESH = pl.DeviceIdType.MESH
F32 = jnp.float32
BF16 = jnp.bfloat16


def mul16(value):
    return pl.multiple_of(value, 16)


def dot(a, b, ca, cb):
    return lax.dot_general(a, b, (((ca,), (cb,)), ((), ())), preferred_element_type=F32)


def chunk_of(width):
    best = 128
    for size in range(128, 1537, 128):
        if width % size == 0:
            best = size
    return best


def wide_of(chips):
    best = 1
    for size in range(1, chips + 1):
        if size * size <= chips and chips % size == 0:
            best = size
    return best


def kernel(
    n_dp, n_ctx, group, rounds,
    order_hbm, x, w, q_hbm, k, g_hbm,
    o_hbm, dq_hbm, dk_hbm, fin_hbm,
    o, dq, dk, fin, order, q, g, x2, w_all, k_all, v_all, probs, dv_acc, dv_sib, dk_acc, dvf, dkf, dv2, term, term_r, last_s, last_r, z_s, z_r,
    send_sem, recv_sem, local_sem,
):
    rows, width = x.shape
    shard, hd = w.shape
    heads = q.shape[1] // hd
    scale = 1.0 / hd**0.5
    chips = n_dp // 2
    pieces = max(rounds, 1) * (n_ctx if rounds else 1)
    part = shard // pieces
    aligned = shard % 128 == 0
    me = lax.axis_index("dp")
    z = lax.axis_index("ctx")
    chip, core = me // 2, lax.rem(me, 2)
    sib = me + 1 - 2 * core
    nxt = lax.rem(z + 1, n_ctx)
    prev = lax.rem(z + n_ctx - 1, n_ctx)

    wide = wide_of(chips)
    tall = chips // wide
    down, across = chip // wide, lax.rem(chip, wide)

    def device(i, j):
        return 2 * (lax.rem(down + tall + i, tall) * wide + lax.rem(across + wide + j, wide)) + core

    sides = [(0, j) for j in range(1, wide)]
    heights = [(i, 0) for i in range(1, tall)]
    others = [(i, j) for i in range(tall) for j in range(wide) if i or j]

    count = [0]
    sent = []

    def send(src, dst, target):
        at = count[0]
        count[0] += 1
        copy = pltpu.make_async_remote_copy(
            src_ref=src, dst_ref=dst, send_sem=send_sem.at[at], recv_sem=recv_sem.at[at],
            device_id=target, device_id_type=MESH,
        )
        copy.start()
        sent.append(copy)
        return at

    def arrived(ref, at):
        pltpu.make_async_remote_copy(
            src_ref=ref, dst_ref=ref, send_sem=send_sem.at[at], recv_sem=recv_sem.at[at],
            device_id={"dp": sib}, device_id_type=MESH,
        ).wait_recv()

    own = pl.ds(mul16(me * shard), shard)
    pairs = [
        (order_hbm, order), (k, k_all.at[pl.ds(0, rows)]), (q_hbm, q), (g_hbm, g),
        (x, x2.at[pl.ds(0, rows)]), (w, w_all.at[own]),
    ]
    loads = [
        pltpu.make_async_copy(src, dst, local_sem.at[i]) for i, (src, dst) in enumerate(pairs)
    ]
    for load in loads:
        load.start()

    barrier = pltpu.get_barrier_semaphore()
    near = sides + heights
    for i, j in near:
        pl.semaphore_signal(barrier, inc=1, device_id={"dp": device(i, j)}, device_id_type=MESH)
    pl.semaphore_signal(barrier, inc=1, device_id={"dp": sib}, device_id_type=MESH)
    for off in range(1, n_ctx):
        pl.semaphore_signal(
            barrier, inc=1, device_id={"ctx": lax.rem(z + off, n_ctx)}, device_id_type=MESH
        )
    pl.semaphore_signal(barrier, inc=1, device_id={"dp": sib, "ctx": nxt}, device_id_type=MESH)
    pl.semaphore_signal(barrier, inc=1, device_id={"dp": sib, "ctx": prev}, device_id_type=MESH)
    pl.semaphore_wait(barrier, len(near) + n_ctx + 2)

    keys_at = send(k, k_all.at[pl.ds(rows, rows)], {"ctx": nxt})
    half = shard // 2 if shard % 32 == 0 else shard
    halves = [(0, half, sides, heights)]
    if half < shard:
        halves.append((half, half, heights, sides))

    def w_rows(index, start, size):
        return w_all.at[pl.ds(mul16(index * shard + start), size)]

    w_at = {}

    def send_w(start, size, i, j, di, dj):
        src = w.at[pl.ds(start, size)] if not (i or j) else w_rows(device(-i, -j), start, size)
        dst = w_rows(device(-i, -j), start, size)
        w_at[start, i + di, j + dj] = send(src, dst, {"dp": device(di, dj)})

    for start, size, early, late in halves:
        for i, j in early:
            send_w(start, size, 0, 0, i, j)
    for start, size, early, late in halves:
        for i, j in late:
            send_w(start, size, 0, 0, i, j)
    w_sib_at = {}
    for start, size, early, late in halves:
        src = w.at[pl.ds(start, size)]
        w_sib_at[start, 0, 0] = send(src, w_rows(me, start, size), {"dp": sib})
    x_at = []
    if aligned:
        for j in range(chips):
            cols = pl.ds(pl.multiple_of((2 * j + 1 - core) * shard, 128), shard)
            x_at.append(send(x.at[:, cols], x2.at[pl.ds(rows, rows), cols], {"dp": sib}))
    else:
        x_at.append(send(x, x2.at[pl.ds(rows, rows)], {"dp": sib}))
    loads[0].wait()

    per = order.shape[0] // n_ctx
    blk = rows // per
    key_row = lax.broadcasted_iota(jnp.int32, (2 * rows, rows), 0)
    q_row = lax.broadcasted_iota(jnp.int32, (2 * rows, rows), 1)
    key_place = key_row
    q_place = q_row
    for b in range(per):
        mine = order[z * per + b]
        q_place = jnp.where(q_row >= b * blk, q_row + (mine - b) * blk, q_place)
    for b in range(2 * per):
        owner = z if b < per else prev
        block = order[owner * per + b % per]
        key_place = jnp.where(key_row >= b * blk, key_row + (block - b) * blk, key_place)
    hidden = jnp.where(key_place <= q_place, 0.0, 1.0).astype(F32)
    hidden = jnp.concatenate([hidden] * group, axis=1)

    def stacked(ref, it):
        return jnp.concatenate(
            [
                ref[:, pl.ds((it * group + i) * hd, hd)]
                for i in range(group)
            ],
            axis=0,
        )

    for load in loads[1:4]:
        load.wait()
    arrived(k_all.at[pl.ds(rows, rows)], keys_at)
    dv_acc[...] = jnp.zeros_like(dv_acc)
    dk_acc[...] = jnp.zeros_like(dk_acc)

    def first(it, carry):
        scores = dot(k_all[...], stacked(q, it), 1, 1) * scale
        scores = jnp.where(hidden > 0.0, -1e30, scores)
        top = jnp.max(scores, axis=0, keepdims=True)
        weights = jnp.exp(scores - top)
        prob = weights * (1.0 / jnp.sum(weights, axis=0, keepdims=True))
        probs[it] = prob
        dv_acc[...] += dot(prob.astype(BF16), stacked(g, it), 1, 0)
        return carry

    for it in range(heads // group):
        first(it, 0)

    def w_came(start, size, i, j):
        came = w_rows(device(-i, -j), start, size)
        arrived(came, w_at[start, i, j])
        w_sib_at[start, i, j] = send(came, came, {"dp": sib})

    dvf[0] = dv_acc[pl.ds(rows, rows)].astype(BF16)
    at = send(dvf.at[0], dvf.at[1], {"ctx": prev})
    sib_far_at = send(dvf.at[0], dvf.at[2], {"dp": sib, "ctx": prev})
    sib_own_at = send(dv_acc.at[pl.ds(0, rows)], dv_sib, {"dp": sib})
    for start, size, early, late in halves:
        for i, j in early:
            arrived(w_rows(device(-i, -j), start, size), w_at[start, i, j])
            for di, dj in late:
                send_w(start, size, i, j, di, dj)
            came = w_rows(device(-i, -j), start, size)
            w_sib_at[start, i, j] = send(came, came, {"dp": sib})
    loads[4].wait()
    arrived(dvf.at[1], at)
    dv2[pl.ds(0, rows)] = (dv_acc[pl.ds(0, rows)] + dvf[1].astype(F32)).astype(BF16)
    for j in range(len(x_at)):
        if aligned:
            cols = pl.ds(pl.multiple_of((2 * j + core) * shard, 128), shard)
            arrived(x2.at[pl.ds(rows, rows), cols], x_at[j])
        else:
            arrived(x2.at[pl.ds(rows, rows)], x_at[j])
    arrived(dv_sib, sib_own_at)
    arrived(dvf.at[2], sib_far_at)
    dv2[pl.ds(rows, rows)] = (dv_sib[...] + dvf[2].astype(F32)).astype(BF16)

    def shard_term(index):
        cols = pl.ds(pl.multiple_of(index * shard, 128), shard)
        term[pl.ds(mul16(index * shard), shard)] = dot(x2[:, cols], dv2[...], 0, 0).astype(BF16)

    if aligned:
        for i, j in others:
            shard_term(device(i, j))
    else:
        size = chunk_of(width)
        for start in range(0, width, size):
            cols = pl.ds(start, size)
            term[cols] = dot(x2[:, cols], dv2[...], 0, 0).astype(BF16)
    def piece(index):
        if not rounds:
            return 0
        return (index // n_ctx) * n_ctx + lax.rem(z + 1 + index % n_ctx, n_ctx)

    def piece_rows(index):
        return pl.ds(mul16(piece(index) * part), part)

    def lanes(index):
        return (sides, heights) if index % 2 == 0 else (heights, sides)

    def term_rows(index, i, j):
        return term.at[pl.ds(mul16(device(i, j) * shard + piece(index) * part), part)]

    term_at = []
    for index in range(pieces):
        early, late = lanes(index)
        there = piece_rows(index)
        line = {}
        for n, (i, j) in enumerate(late + [(0, 0)]):
            for m, (di, dj) in enumerate(early):
                line[n, m] = send(
                    term_rows(index, i + di, j + dj), term_r.at[m, n, there], {"dp": device(di, dj)}
                )
        term_at.append(line)

    last_at = []

    def pass_piece(index):
        early, late = lanes(index)
        there = piece_rows(index)
        line = []
        for n, (i, j) in enumerate(late):
            total = term_rows(index, i, j)[...].astype(F32)
            for m in range(len(early)):
                arrived(term_r.at[m, n, there], term_at[index][n, m])
                total += term_r[m, n, there].astype(F32)
            last_s[n, there] = total.astype(BF16)
            line.append(send(last_s.at[n, there], last_r.at[n, there], {"dp": device(i, j)}))
        last_at.append(line)

    loads[5].wait()
    for start, size, early, late in halves:
        for i, j in late:
            w_came(start, size, i, j)
        for i, j in others:
            if i and j:
                w_came(start, size, i, j)
    for start, size, early, late in halves:
        for i, j in [(0, 0)] + others:
            arrived(w_rows(device(-i, -j) + 1 - 2 * core, start, size), w_sib_at[start, i, j])
    v_own = pl.ds(0, rows)
    v_far = pl.ds(rows, rows)
    size = chunk_of(width)

    total = jnp.zeros((rows, hd), F32)
    for start in range(0, width, size):
        cols = pl.ds(start, size)
        total = total + dot(x2[pl.ds(0, rows), cols], w_all[cols], 1, 0)
    v_all[v_own] = total.astype(BF16)
    at = send(v_all.at[v_own], v_all.at[v_far], {"ctx": nxt})

    z_at = []

    def finish_piece(index):
        there = piece_rows(index)
        total = term[pl.ds(mul16(me * shard + piece(index) * part), part)].astype(F32)
        early, late = lanes(index)
        for m in range(len(early)):
            arrived(term_r.at[m, len(late), there], term_at[index][len(late), m])
            total += term_r[m, len(late), there].astype(F32)
        for n in range(len(late)):
            arrived(last_r.at[n, there], last_at[index][n])
            total += last_r[n, there].astype(F32)
        if not rounds:
            z_s[...] = total.astype(BF16)
            z_r[0, z] = z_s[...]
            for off in range(1, n_ctx):
                z_at.append(send(z_s, z_r.at[0, z], {"ctx": lax.rem(z + off, n_ctx)}))
            return
        turn, step = index // n_ctx, index % n_ctx
        if step < n_ctx - 1:
            z_s[there] = total.astype(BF16)
            target = {"ctx": lax.rem(z + 1 + step, n_ctx)}
            z_at.append(send(z_s.at[there], z_r.at[turn, z], target))
        else:
            z_r[turn, z] = total.astype(BF16)

    f_at = []

    def finish_round(turn):
        for off in range(1, n_ctx):
            at = z_at[turn * (n_ctx - 1) + off - 1]
            arrived(z_r.at[turn, lax.rem(z + n_ctx - off, n_ctx)], at)
        total = z_r[turn, 0].astype(F32)
        for index in range(1, n_ctx):
            total += z_r[turn, index].astype(F32)
        if not rounds:
            fin[...] = total.astype(BF16)
            return
        mine = pl.ds(mul16((turn * n_ctx + z) * part), part)
        fin[mine] = total.astype(BF16)
        for off in range(1, n_ctx):
            f_at.append(send(fin.at[mine], fin.at[mine], {"ctx": lax.rem(z + off, n_ctx)}))

    if aligned:
        shard_term(me)
    for index in range(min(4, pieces)):
        pass_piece(index)
    arrived(v_all.at[v_far], at)
    v_t = v_all[...].T
    k_t = k_all[...].T

    def second(it, carry):
        prob = probs[it]
        q_rows = stacked(q, it)
        out_t = dot(v_t, prob.astype(BF16), 1, 0)
        dprob = dot(v_all[...], stacked(g, it), 1, 1)
        delta = jnp.sum(prob * dprob, axis=0, keepdims=True)
        dscore = (prob * (dprob - delta)).astype(BF16)
        dk_acc[...] += dot(dscore, q_rows, 1, 0)
        dq_t = dot(k_t, dscore, 1, 0) * scale
        for i in range(group):
            cols = pl.ds((it * group + i) * hd, hd)
            o[:, cols] = out_t[:, i * rows:(i + 1) * rows].astype(BF16).T
            dq[:, cols] = dq_t[:, i * rows:(i + 1) * rows].astype(BF16).T
        return carry

    steps = heads // group
    jobs = [functools.partial(pass_piece, index) for index in range(4, pieces)]
    for index in range(pieces):
        jobs.append(functools.partial(finish_piece, index))
        if index + 1 == n_ctx and rounds:
            jobs.append(functools.partial(finish_round, 0))
    done = 0
    for it in range(steps):
        second(it, 0)
        upto = 3 * (it + 1)
        for job in jobs[done:upto]:
            job()
        done = min(upto, len(jobs))
    stores = [
        pltpu.make_async_copy(src, dst, local_sem.at[i])
        for i, (src, dst) in enumerate([(o, o_hbm), (dq, dq_hbm), (dk, dk_hbm), (fin, fin_hbm)])
    ]
    stores[0].start()
    stores[1].start()
    dkf[0] = (dk_acc[pl.ds(rows, rows)] * scale).astype(BF16)
    dk_at = send(dkf.at[0], dkf.at[1], {"ctx": prev})
    for job in jobs[done:]:
        job()
    if not rounds:
        finish_round(0)
    arrived(dkf.at[1], dk_at)
    dk[...] = (dk_acc[pl.ds(0, rows)] * scale + dkf[1].astype(F32)).astype(BF16)
    stores[2].start()
    for turn in range(1, rounds):
        finish_round(turn)
    for turn in range(rounds):
        for off in range(1, n_ctx):
            index = turn * n_ctx + lax.rem(z + n_ctx - off, n_ctx)
            theirs = pl.ds(mul16(index * part), part)
            arrived(fin.at[theirs], f_at[turn * (n_ctx - 1) + off - 1])
    stores[3].start()
    for copy in sent:
        copy.wait_send()
    for copy in stores:
        copy.wait()


def finish(o, dq, dk, fin, o_out, dq_out, dk_out, gw, o_v, dq_v, dk_v, narrow, wide, sem):
    ins = [(fin, narrow), (o, o_v), (dq, dq_v), (dk, dk_v)]
    outs = [(wide, gw), (o_v, o_out), (dq_v, dq_out), (dk_v, dk_out)]
    loads = [pltpu.make_async_copy(src, dst, sem.at[i]) for i, (src, dst) in enumerate(ins)]
    stores = [pltpu.make_async_copy(src, dst, sem.at[4 + i]) for i, (src, dst) in enumerate(outs)]
    for load in loads:
        load.start()
    for index in range(4):
        loads[index].wait()
        if index == 0:
            wide[...] = narrow[...].astype(F32)
        stores[index].start()
    for store in stores:
        store.wait()


def shards(n_dp, n_ctx, inputs, block_order, w_value, query, keys, out_grad):
    x, q, k, g = inputs[0], query[0], keys[0], out_grad[0]
    rows, width = x.shape
    shard, hd = w_value.shape
    heads = q.shape[1] // hd
    group = 4 if heads % 4 == 0 else 1
    rounds = 0
    for turns in (1, 2):
        if shard % (16 * n_ctx * turns) == 0:
            rounds = turns
    pieces = max(rounds, 1) * (n_ctx if rounds else 1)
    part = shard // pieces
    chips = n_dp // 2
    most = chips // wide_of(chips)
    copies = 5 * chips + 16 + 2 * chips * pieces + 4 * n_ctx
    hbm = pl.BlockSpec(memory_space=pltpu.HBM)
    o, dq, dk, fin = pl.pallas_call(
        functools.partial(kernel, n_dp, n_ctx, group, rounds),
        out_shape=(
            jax.ShapeDtypeStruct(q.shape, BF16),
            jax.ShapeDtypeStruct(q.shape, BF16),
            jax.ShapeDtypeStruct(k.shape, BF16),
            jax.ShapeDtypeStruct(w_value.shape, BF16),
        ),
        in_specs=[hbm] * 6,
        out_specs=(hbm,) * 4,
        scratch_shapes=[
            pltpu.VMEM(q.shape, BF16),
            pltpu.VMEM(q.shape, BF16),
            pltpu.VMEM(k.shape, BF16),
            pltpu.VMEM((shard, hd), BF16),
            pltpu.SMEM(block_order.shape, jnp.int32),
            pltpu.VMEM(q.shape, BF16),
            pltpu.VMEM(g.shape, BF16),
            pltpu.VMEM((2 * rows, width), BF16),
            pltpu.VMEM((width, hd), BF16),
            pltpu.VMEM((2 * rows, hd), BF16),
            pltpu.VMEM((2 * rows, hd), BF16),
            pltpu.VMEM((heads // group, 2 * rows, group * rows), F32),
            pltpu.VMEM((2 * rows, hd), F32),
            pltpu.VMEM((rows, hd), F32),
            pltpu.VMEM((2 * rows, hd), F32),
            pltpu.VMEM((3, rows, hd), BF16),
            pltpu.VMEM((2, rows, hd), BF16),
            pltpu.VMEM((2 * rows, hd), BF16),
            pltpu.VMEM((width, hd), BF16),
            pltpu.VMEM((most, most, shard, hd), BF16),
            pltpu.VMEM((most, shard, hd), BF16),
            pltpu.VMEM((most, shard, hd), BF16),
            pltpu.VMEM((shard, hd), BF16),
            pltpu.VMEM((max(rounds, 1), n_ctx, part, hd), BF16),
            pltpu.SemaphoreType.DMA((copies,)),
            pltpu.SemaphoreType.DMA((copies,)),
            pltpu.SemaphoreType.DMA((6,)),
        ],
        compiler_params=pltpu.CompilerParams(
            collective_id=0, has_side_effects=True, vmem_limit_bytes=60 * 2**20
        ),
    )(block_order, x, w_value, q, k, g)
    return pl.pallas_call(
        finish,
        out_shape=(
            jax.ShapeDtypeStruct(query.shape, BF16),
            jax.ShapeDtypeStruct(query.shape, BF16),
            jax.ShapeDtypeStruct(keys.shape, BF16),
            jax.ShapeDtypeStruct(w_value.shape, F32),
        ),
        in_specs=[hbm] * 4,
        out_specs=(hbm,) * 4,
        scratch_shapes=[
            pltpu.VMEM(query.shape, BF16),
            pltpu.VMEM(query.shape, BF16),
            pltpu.VMEM(keys.shape, BF16),
            pltpu.VMEM((shard, hd), BF16),
            pltpu.VMEM((shard, hd), F32),
            pltpu.SemaphoreType.DMA((8,)),
        ],
        compiler_params=pltpu.CompilerParams(vmem_limit_bytes=60 * 2**20),
    )(o[None], dq[None], dk[None], fin)


def solution(mesh):
    split = P("dp", "ctx", None)
    return jax.shard_map(
        functools.partial(shards, mesh.shape["dp"], mesh.shape["ctx"]),
        mesh=mesh,
        in_specs=(split, P(), P("dp", None), split, split, split),
        out_specs=(split, split, split, P("dp", None)),
        check_vma=False,
    )
```
